32 devices in a mesh: parts: 2 (over y), slab: 4 (over z), valley: 2 (over x), blk: 2 (over core).
Axes of the slice: x: 2, y: 2, z: 4, core: 2. Of those that a mesh axis runs over, the one named last changes fastest.
Arguments:
- potential: bfloat16 [64, 2048], P('slab'), may hold values from -3.5 to 4
- mode_density: bfloat16 [4, 2048, 2048], P(('parts', 'valley'), 'blk'), parts along dimension 0, may hold values from 0 to 1, as said below
- energy: float32 [4], P(('parts', 'valley')), parts along dimension 0, may hold values from -0.5 to 0.5
- hopping: float32 [4], P(('parts', 'valley')), parts along dimension 0, may hold values from 0.6 to 1.4
- mode_energy: float32 [4, 2048], P(('parts', 'valley'), 'blk'), parts along dimension 0, may hold values from -2.5 to 3
- broadening: float32 [4, 2048], P(('parts', 'valley'), 'blk'), parts along dimension 0, may hold values from 0.0078125 to 0.3
- self_left: float32 [4, 2, 2048], P(('parts', 'valley'), None, 'blk'), parts along dimension 0, may hold values from -1 to 1, as said below
- self_right: float32 [4, 2, 2048], P(('parts', 'valley'), None, 'blk'), parts along dimension 0, may hold values from -1 to 1, as said below
- occupation: float32 [4], P(('parts', 'valley')), parts along dimension 0, may hold values from 0.5 to 1.5
Outputs:
- mode_charge: float32 [4, 64, 2048], P(('parts', 'valley'), 'slab', 'blk'), parts along dimension 0
- electron_density: float32 [128, 2048], P(('parts', 'slab'), ('valley', 'blk')), parts along dimension 0
The draws below stay inside these ranges and needn't reach their ends.
There are 2 independent parts, one for each index of `parts`. The reference program is written for one: setup_inputs(seed, part) draws one part's arguments, and reference() takes and returns one part's arrays. A program takes and returns all parts, laid end to end along the dimension named above; an argument that names none is the same for every part. Nothing has to cross between parts.
Inputs may be any that keep to these rules, and one draw needn't show every extreme that they name: `mode_density`: every entry is positive. `self_left`: the imaginary parts (index 1 of the second dimension) are negative. `self_right`: the imaginary parts (index 1 of the second dimension) are negative.
All inputs are finite; a program needn't handle non-finite values.
Results may differ from the reference program's by a relative error of at most 0.0065.
Values sent between devices are 32-bit elements; how exact they have to be, the bound alone decides.
No kernel may reach another device: no remote copies, remote signals or barrier semaphores. Data moves between devices by JAX's collectives and lax.ppermute only.
A program may use at most 64 MiB of HBM per device.

```python
import math
import jax
import jax.numpy as jnp
from jax import lax

WIDTH = 2048
CHAIN = 64
ITEMS = 2


def smooth_bump(places, lower, upper, edge):
    return 0.5 * (jnp.tanh((places - lower) / edge) - jnp.tanh((places - upper) / edge))


def draw_potential(key, part):
    first_key = jax.random.fold_in(key, 17)
    places = (jnp.arange(CHAIN, dtype=jnp.float32) + 0.5) / CHAIN
    edge = 2.0 / CHAIN
    parity = 1.0 - 2.0 * (jnp.arange(CHAIN, dtype=jnp.int32) % 2).astype(jnp.float32)
    double_bump = smooth_bump(places, 0.3, 0.38, edge) + smooth_bump(places, 0.62, 0.7, edge)
    barrier = 0.4 * double_bump
    roughness = jax.random.uniform(first_key, (CHAIN, WIDTH), jnp.float32, -0.6, 0.6)
    row_level = barrier + 2.5 * parity
    return (row_level[:, None] + roughness).astype(jnp.bfloat16)


def draw_mode_density(key, part):
    first_key = jax.random.fold_in(key, 29)
    uniform_part = jax.random.uniform(first_key, (ITEMS, WIDTH, WIDTH), jnp.float32, 0.0, 1.0)
    factors = uniform_part ** 24 + 0.0001
    return (factors / jnp.sum(factors, axis=-1, keepdims=True)).astype(jnp.bfloat16)


def contact_energy(key):
    first_key, second_key = jax.random.split(key)
    real_part = jax.random.uniform(first_key, (ITEMS, WIDTH), jnp.float32, -0.8, 0.8)
    imag_part = -jax.random.uniform(second_key, (ITEMS, WIDTH), jnp.float32, 0.1, 0.9)
    return jnp.stack([real_part, imag_part], axis=1)


def draw_self_left(key, part):
    return contact_energy(jax.random.fold_in(key, 3))


def draw_self_right(key, part):
    return contact_energy(jax.random.fold_in(key, 5))


def level_of(own_key, extent, pieces, least, largest):
    loudness = 1.0
    for axis_at, parts in pieces:
        draws = jax.random.uniform(jax.random.fold_in(jax.random.fold_in(own_key, 6), axis_at), (parts,), jnp.float32, least / len(pieces), largest / len(pieces))
        loudness = loudness * jnp.repeat(jnp.exp(draws), extent[axis_at] // parts).reshape((-1,) + (1,) * (len(extent) - 1 - axis_at))
    return loudness


def setup_inputs(seed: int = 0, part: int = 0) -> dict:
    arg_keys = jax.random.split(jax.random.key(seed), 10)
    part_splits = jax.random.split(jax.random.fold_in(arg_keys[9], part), 10)
    return {
        "potential": draw_potential(jax.random.fold_in(arg_keys[9], 71), part),
        "mode_density": draw_mode_density(jax.random.fold_in(jax.random.fold_in(arg_keys[9], part), 71), part),
        "energy": jnp.clip(jax.random.uniform(part_splits[2], (ITEMS,), jnp.float32, -0.5, 0.5) * level_of(part_splits[2], (ITEMS,), ((0, 2),), -0.4, 0.0), -0.5, 0.5),
        "hopping": jnp.clip(0.6 + 0.79999995 * jax.random.uniform(part_splits[3], (ITEMS,), jnp.float32) ** level_of(part_splits[3], (ITEMS,), ((0, 2),), -0.2, 0.2), 0.6, 1.4),
        "mode_energy": jnp.clip(-2.5 + 5.5 * jax.random.uniform(part_splits[4], (ITEMS, WIDTH), jnp.float32) ** level_of(part_splits[4], (ITEMS, WIDTH), ((0, 2), (1, 2)), -0.2, 0.2), -2.5, 3.0),
        "broadening": jnp.clip(jnp.exp(math.log(0.3) - 3.6480575 * jax.random.uniform(part_splits[5], (ITEMS, WIDTH), jnp.float32) ** level_of(part_splits[5], (ITEMS, WIDTH), ((0, 2), (1, 2)), -0.2, 0.2)), 0.0078125, 0.3),
        "self_left": draw_self_left(jax.random.fold_in(jax.random.fold_in(arg_keys[9], part), 71), part),
        "self_right": draw_self_right(jax.random.fold_in(jax.random.fold_in(arg_keys[9], part), 71), part),
        "occupation": jnp.clip(0.5 + 1.0 * jax.random.uniform(part_splits[8], (ITEMS,), jnp.float32) ** level_of(part_splits[8], (ITEMS,), ((0, 2),), -0.2, 0.2), 0.5, 1.5),
    }


def reference(potential, mode_density, energy, hopping, mode_energy, broadening, self_left, self_right, occupation):
    profile = mode_density.astype(jnp.float32)
    projected = jnp.einsum("inx,sx->isn", profile, potential.astype(jnp.float32))
    onsite_re = energy[:, None, None] - mode_energy[:, None, :] - projected
    onsite_im = jnp.broadcast_to(broadening[:, None, :], projected.shape)
    hop_square = (hopping * hopping)[:, None]

    def sweep(carried, slab_onsite):
        carried_re, carried_im = carried
        slab_re, slab_im = slab_onsite
        bottom_re = slab_re - carried_re
        bottom_im = slab_im - carried_im
        magnitude = bottom_re * bottom_re + bottom_im * bottom_im
        next_re = hop_square * bottom_re / magnitude
        next_im = -hop_square * bottom_im / magnitude
        return (next_re, next_im), (carried_re, carried_im)

    slab_major = (jnp.moveaxis(onsite_re, 1, 0), jnp.moveaxis(onsite_im, 1, 0))
    final_left, (left_re, left_im) = lax.scan(sweep, (self_left[:, 0, :], self_left[:, 1, :]), slab_major)
    final_right, (right_re, right_im) = lax.scan(sweep, (self_right[:, 0, :], self_right[:, 1, :]), slab_major, reverse=True)
    bottom_re = onsite_re - jnp.moveaxis(left_re + right_re, 0, 1)
    bottom_im = onsite_im - jnp.moveaxis(left_im + right_im, 0, 1)
    charge = occupation[:, None, None] / math.pi * bottom_im / (bottom_re * bottom_re + bottom_im * bottom_im)
    charge_half = lax.optimization_barrier(charge.astype(jnp.bfloat16)).astype(jnp.float32)
    density = jnp.einsum("isn,inx->sx", charge_half, profile)
    return charge, density
```

```python
import math

import jax
import jax.numpy as jnp
from jax import lax
from jax.experimental import pallas as pl
from jax.experimental.pallas import tpu as pltpu
from jax.sharding import PartitionSpec as P

LANES = 128
VMEM_LIMIT = 24 * 1024 * 1024


def times(first, second):
    return (
        first[0] * second[0] - first[1] * second[1],
        first[0] * second[1] + first[1] * second[0],
    )


def plus(first, second):
    return first[0] + second[0], first[1] + second[1]


def minus(first, second):
    return first[0] - second[0], first[1] - second[1]


def invert(value):
    scale = 1.0 / (value[0] * value[0] + value[1] * value[1])
    return value[0] * scale, -(value[1] * scale)


def one_minus(value):
    return 1.0 - value[0], -value[1]


def extend(run, slab):
    low, high, through = run
    grown = invert(minus(slab, high))
    return (
        plus(low, times(through, grown)),
        grown,
        times(through, times(grown, grown)),
    )


def join(first, second):
    low1, high1, through1 = first
    low2, high2, through2 = second
    bridge = invert(one_minus(times(high1, low2)))
    return (
        plus(low1, times(times(through1, low2), bridge)),
        plus(high2, times(times(through2, high1), bridge)),
        times(times(through1, through2), times(bridge, bridge)),
    )


def flip(run):
    return run[1], run[0], run[2]


def carry(run, value):
    low, high, through = run
    return plus(high, times(times(through, value), invert(one_minus(times(low, value)))))


def pick(flag, chosen, otherwise):
    return jax.tree.map(lambda a, b: jnp.where(flag, a, b), chosen, otherwise)


def pack(run):
    return jnp.stack([part for pair in run for part in pair])


def unpack(stack):
    return tuple((stack[2 * k], stack[2 * k + 1]) for k in range(stack.shape[0] // 2))


def fold_row(row, fold):
    for group in range(fold.shape[0]):
        fold[group : group + 1, :] = row[:, group * LANES : (group + 1) * LANES]
    return fold[...]


def project_kernel(
    energy,
    hopping,
    potential,
    mode_energy,
    broadening,
    self_left,
    self_right,
    profile_hbm,
    onsite_out,
    contact_out,
    run_out,
    profile,
    staged,
    fold,
    arrived,
):
    slabs = potential.shape[0]
    groups = profile.shape[0] // LANES
    copies = []
    for group in range(groups):
        rows = pl.ds(group * LANES, LANES)
        copies.append(
            pltpu.make_async_copy(profile_hbm.at[0, rows], profile.at[rows], arrived.at[group])
        )
        copies[-1].start()
    inverse = 1.0 / jnp.full((groups, LANES), hopping[0], jnp.float32)
    level = (energy[0] - fold_row(mode_energy, fold.at[0])) * inverse
    damping = fold_row(broadening, fold.at[1]) * inverse
    for part in range(2):
        contact_out[part] = fold_row(self_left.at[0, part : part + 1], fold.at[2 + part]) * inverse
        contact_out[2 + part] = (
            fold_row(self_right.at[0, part : part + 1], fold.at[4 + part]) * inverse
        )
    for group in range(groups):
        copies[group].wait()
        staged[group * slabs : (group + 1) * slabs, :] = lax.dot_general(
            potential[...],
            profile[group * LANES : (group + 1) * LANES, :],
            (((1,), (1,)), ((), ())),
            preferred_element_type=jnp.float32,
        )
    runs = []
    length = math.gcd(slabs, 4)
    onsite_out[slabs] = damping
    for start in range(0, slabs, length):
        run = None
        for slab in range(start, start + length):
            real = level - staged[pl.ds(slab, groups, stride=slabs), :] * inverse
            onsite_out[slab] = real
            onsite = (real, damping)
            if run is None:
                alone = invert(onsite)
                run = (alone, alone, times(alone, alone))
            else:
                run = extend(run, onsite)
        runs.append(run)
    while len(runs) > 1:
        paired = [join(runs[k], runs[k + 1]) for k in range(0, len(runs) - 1, 2)]
        runs = paired + runs[2 * len(paired) :]
    for place, part in enumerate(part for pair in runs[0] for part in pair):
        run_out[place] = part


def charge_kernel(
    hopping,
    occupation,
    upper,
    onsite_in,
    outer_in,
    inner_run,
    sent_in,
    profile,
    charge_out,
    density_out,
    staged,
):
    slabs = onsite_in.shape[0] - 1
    groups = onsite_in.shape[1]
    outer = (outer_in[0], outer_in[1])
    inner = carry(
        tuple((inner_run[2 * k], inner_run[2 * k + 1]) for k in range(3)), (sent_in[0], sent_in[1])
    )
    is_upper = upper[0] > 0
    left = pick(is_upper, inner, outer)
    right = pick(is_upper, outer, inner)
    damping = onsite_in[slabs]
    weight = jnp.full((groups, LANES), occupation[0], jnp.float32) / (
        jnp.full((groups, LANES), hopping[0], jnp.float32) * math.pi
    )
    lefts, rights = [left], [right]
    for slab in range(slabs - 1):
        lefts.append(invert(minus((onsite_in[slab], damping), lefts[-1])))
        rights.append(invert(minus((onsite_in[slabs - 1 - slab], damping), rights[-1])))
    for slab in range(slabs):
        below = minus((onsite_in[slab], damping), plus(lefts[slab], rights[slabs - 1 - slab]))
        staged[pl.ds(slab, groups, stride=slabs), :] = (
            weight * below[1] / (below[0] * below[0] + below[1] * below[1])
        )
    for group in range(groups):
        charge_out[0, :, group * LANES : (group + 1) * LANES] = staged[
            group * slabs : (group + 1) * slabs, :
        ]
    half = charge_out[0].astype(jnp.bfloat16)
    width = density_out.shape[1]
    step = math.gcd(width, 256)
    for start in range(0, width, step):
        density_out[:, start : start + step] = jnp.dot(
            half, profile[0, :, start : start + step], preferred_element_type=jnp.float32
        )


def body(
    potential,
    mode_density,
    energy,
    hopping,
    mode_energy,
    broadening,
    self_left,
    self_right,
    occupation,
):
    slabs, width = potential.shape
    modes = mode_density.shape[1]
    groups = modes // LANES
    smem = pl.BlockSpec(memory_space=pltpu.SMEM)
    vmem = pl.BlockSpec(memory_space=pltpu.VMEM)
    anywhere = pl.BlockSpec(memory_space=pl.ANY)
    f32 = jnp.float32
    onsite, contact, run = pl.pallas_call(
        project_kernel,
        out_shape=(
            jax.ShapeDtypeStruct((slabs + 1, groups, LANES), f32),
            jax.ShapeDtypeStruct((4, groups, LANES), f32),
            jax.ShapeDtypeStruct((6, groups, LANES), f32),
        ),
        in_specs=[smem, smem, vmem, vmem, vmem, vmem, vmem, anywhere],
        out_specs=(vmem, vmem, vmem),
        scratch_shapes=[
            pltpu.VMEM((modes, width), jnp.bfloat16),
            pltpu.VMEM((groups * slabs, LANES), f32),
            pltpu.VMEM((6, groups, LANES), f32),
            pltpu.SemaphoreType.DMA((groups,)),
        ],
        compiler_params=pltpu.CompilerParams(vmem_limit_bytes=VMEM_LIMIT),
        cost_estimate=pl.CostEstimate(
            flops=2 * slabs * width * modes, bytes_accessed=2 * width * modes, transcendentals=0
        ),
    )(energy, hopping, potential, mode_energy, broadening, self_left, self_right, mode_density)

    count = lax.axis_size("slab")
    place = lax.axis_index("slab")
    group = unpack(run)
    zero = jnp.zeros((groups, LANES), f32)
    nothing = ((zero, zero), (zero, zero), (zero + 1.0, zero))
    before, after = nothing, nothing
    left_end, right_end = unpack(contact)
    reach = 1
    while 2 * reach < count:
        pairs = [(k, k ^ reach) for k in range(count)]
        other = unpack(lax.ppermute(pack(group), "slab", pairs))
        is_second = (place & reach) > 0
        if reach == 1:
            before, after = pick(is_second, other, nothing), pick(is_second, nothing, other)
        else:
            before, after = (
                pick(is_second, join(other, before), before),
                pick(is_second, after, join(after, other)),
            )
        group = join(pick(is_second, other, group), pick(is_second, group, other))
        reach *= 2
    is_upper = (place & reach) > 0
    end = pick(is_upper, right_end, left_end)
    if count > 1:
        sent = pack((carry(pick(is_upper, flip(group), group), end),))
        sent = lax.ppermute(sent, "slab", [(k, k ^ reach) for k in range(count)])
    else:
        sent = pack((right_end,))
    outer = pack((carry(pick(is_upper, flip(after), before), end),))
    inner_run = pack(pick(is_upper, before, flip(after)))
    upper = is_upper.astype(jnp.int32).reshape(1)

    charge, density = pl.pallas_call(
        charge_kernel,
        out_shape=(
            jax.ShapeDtypeStruct((1, slabs, modes), f32),
            jax.ShapeDtypeStruct((slabs, width), f32),
        ),
        in_specs=[smem, smem, smem, vmem, vmem, vmem, vmem, vmem],
        out_specs=(vmem, vmem),
        scratch_shapes=[pltpu.VMEM((groups * slabs, LANES), f32)],
        compiler_params=pltpu.CompilerParams(vmem_limit_bytes=VMEM_LIMIT),
        cost_estimate=pl.CostEstimate(
            flops=2 * slabs * width * modes, bytes_accessed=2 * width * modes, transcendentals=0
        ),
    )(hopping, occupation, upper, onsite, outer, inner_run, sent, mode_density)

    valleys, blocks = lax.axis_size("valley"), lax.axis_size("blk")
    piece = width // (valleys * blocks)
    terms = density.reshape(slabs, valleys, blocks, piece)
    for name, axis in (("blk", 2), ("valley", 1)):
        number, index = lax.axis_size(name), lax.axis_index(name)
        total = lax.dynamic_index_in_dim(terms, index, axis, keepdims=True)
        for shift in range(1, number):
            away = lax.dynamic_index_in_dim(terms, (index + shift) % number, axis, keepdims=True)
            total = total + lax.ppermute(
                away, name, [(k, (k + shift) % number) for k in range(number)]
            )
        terms = total
    return charge, terms.reshape(slabs, piece)


def solution(mesh):
    placed = (
        P("slab", None),
        P(("parts", "valley"), "blk", None),
        P(("parts", "valley")),
        P(("parts", "valley")),
        P(("parts", "valley"), "blk"),
        P(("parts", "valley"), "blk"),
        P(("parts", "valley"), None, "blk"),
        P(("parts", "valley"), None, "blk"),
        P(("parts", "valley")),
    )
    return jax.shard_map(
        body,
        mesh=mesh,
        in_specs=placed,
        out_specs=(P(("parts", "valley"), "slab", "blk"), P(("parts", "slab"), ("valley", "blk"))),
        check_vma=False,
    )
```

```python
import functools
import math

import jax
import jax.numpy as jnp
from jax import lax
from jax.experimental import pallas as pl
from jax.experimental.pallas import tpu as pltpu
from jax.sharding import PartitionSpec as P

LANES = 128
VMEM_LIMIT = 24 * 1024 * 1024
SMALL_LIMIT = 8 * 1024 * 1024


def times(first, second):
    return (
        first[0] * second[0] - first[1] * second[1],
        first[0] * second[1] + first[1] * second[0],
    )


def plus(first, second):
    return first[0] + second[0], first[1] + second[1]


def minus(first, second):
    return first[0] - second[0], first[1] - second[1]


def invert(value):
    scale = 1.0 / (value[0] * value[0] + value[1] * value[1])
    return value[0] * scale, -(value[1] * scale)


def one_minus(value):
    return 1.0 - value[0], -value[1]


def extend(run, slab):
    low, high, through = run
    grown = invert(minus(slab, high))
    return (
        plus(low, times(through, grown)),
        grown,
        times(through, times(grown, grown)),
    )


def join(first, second):
    low1, high1, through1 = first
    low2, high2, through2 = second
    bridge = invert(one_minus(times(high1, low2)))
    return (
        plus(low1, times(times(through1, low2), bridge)),
        plus(high2, times(times(through2, high1), bridge)),
        times(times(through1, through2), times(bridge, bridge)),
    )


def flip(run):
    return run[1], run[0], run[2]


def carry(run, value):
    low, high, through = run
    return plus(high, times(times(through, value), invert(one_minus(times(low, value)))))


def pick(flag, chosen, otherwise):
    return jax.tree.map(lambda a, b: jnp.where(flag, a, b), chosen, otherwise)


def pack(run):
    return jnp.stack([part for pair in run for part in pair])


def unpack(stack):
    return tuple((stack[2 * k], stack[2 * k + 1]) for k in range(stack.shape[0] // 2))


def fold_row(row, fold):
    for group in range(fold.shape[0]):
        fold[group : group + 1, :] = row[:, group * LANES : (group + 1) * LANES]
    return fold[...]


def project_kernel(
    energy,
    hopping,
    potential_hbm,
    mode_energy_hbm,
    broadening_hbm,
    self_left_hbm,
    self_right_hbm,
    profile_hbm,
    profile,
    onsite_out,
    contact_out,
    run_out,
    potential,
    mode_energy,
    broadening,
    self_left,
    self_right,
    staged,
    fold,
    small_arrived,
    arrived,
):
    slabs = potential.shape[0]
    groups = profile.shape[0] // LANES
    small = []
    for place, (source, target) in enumerate(
        (
            (potential_hbm, potential),
            (mode_energy_hbm, mode_energy),
            (broadening_hbm, broadening),
            (self_left_hbm, self_left),
            (self_right_hbm, self_right),
        )
    ):
        small.append(pltpu.make_async_copy(source, target, small_arrived.at[place]))
        small[-1].start()
    copies = []
    for group in range(groups):
        rows = pl.ds(group * LANES, LANES)
        copies.append(
            pltpu.make_async_copy(profile_hbm.at[0, rows], profile.at[rows], arrived.at[group])
        )
        copies[-1].start()
    for copy in small:
        copy.wait()
    inverse = 1.0 / jnp.full((groups, LANES), hopping[0], jnp.float32)
    level = (energy[0] - fold_row(mode_energy, fold.at[0])) * inverse
    damping = fold_row(broadening, fold.at[1]) * inverse
    onsite_out[slabs] = damping
    onsite_out[slabs + 1] = inverse
    for part in range(2):
        contact_out[part] = fold_row(self_left.at[0, part : part + 1], fold.at[2 + part]) * inverse
        contact_out[2 + part] = (
            fold_row(self_right.at[0, part : part + 1], fold.at[4 + part]) * inverse
        )
    for group in range(groups):
        copies[group].wait()
        staged[group * slabs : (group + 1) * slabs, :] = lax.dot_general(
            potential[...],
            profile[group * LANES : (group + 1) * LANES, :],
            (((1,), (1,)), ((), ())),
            preferred_element_type=jnp.float32,
        )
    runs = []
    length = math.gcd(slabs, 4)
    for start in range(0, slabs, length):
        run = None
        for slab in range(start, start + length):
            real = level - staged[pl.ds(slab, groups, stride=slabs), :] * inverse
            onsite_out[slab] = real
            onsite = (real, damping)
            if run is None:
                alone = invert(onsite)
                run = (alone, alone, times(alone, alone))
            else:
                run = extend(run, onsite)
        runs.append(run)
    while len(runs) > 1:
        paired = [join(runs[k], runs[k + 1]) for k in range(0, len(runs) - 1, 2)]
        runs = paired + runs[2 * len(paired) :]
    for place, part in enumerate(part for pair in runs[0] for part in pair):
        run_out[place] = part


def charge_kernel(
    reach,
    occupation,
    onsite_in,
    outer_in,
    inner_run,
    sent_in,
    profile,
    charge_hbm,
    *rest,
):
    densities, (staged, charge, half, leaving) = rest[:-4], rest[-4:]
    slabs = charge.shape[1]
    groups = onsite_in.shape[1]
    outer = (outer_in[0], outer_in[1])
    inner = carry(
        tuple((inner_run[2 * k], inner_run[2 * k + 1]) for k in range(3)), (sent_in[0], sent_in[1])
    )
    is_upper = (lax.axis_index("slab") & reach) > 0
    left = pick(is_upper, inner, outer)
    right = pick(is_upper, outer, inner)
    damping = onsite_in[slabs]
    weight = (occupation[0] / math.pi) * onsite_in[slabs + 1]
    lefts, rights = [left], [right]
    for slab in range(slabs - 1):
        lefts.append(invert(minus((onsite_in[slab], damping), lefts[-1])))
        rights.append(invert(minus((onsite_in[slabs - 1 - slab], damping), rights[-1])))
    for slab in range(slabs):
        below = minus((onsite_in[slab], damping), plus(lefts[slab], rights[slabs - 1 - slab]))
        staged[pl.ds(slab, groups, stride=slabs), :] = (
            weight * below[1] / (below[0] * below[0] + below[1] * below[1])
        )
    for group in range(groups):
        columns = slice(group * LANES, (group + 1) * LANES)
        rows = staged[group * slabs : (group + 1) * slabs, :]
        charge[0, :, columns] = rows
        half[:, columns] = rows.astype(jnp.bfloat16)
    copy = pltpu.make_async_copy(charge, charge_hbm, leaving)
    copy.start()
    blocks = len(densities)
    block = lax.axis_index("blk")
    valleys, piece = densities[0].shape[0], densities[0].shape[2]
    for shift in reversed(range(blocks)):
        owner = lax.rem(block + shift, blocks)
        for valley in range(valleys):
            start = pl.multiple_of((valley * blocks + owner) * piece, piece)
            densities[shift][valley] = jnp.dot(
                half[...], profile[:, pl.ds(start, piece)], preferred_element_type=jnp.float32
            )
    copy.wait()


def alone_like(run):
    zero = jnp.zeros_like(run[0])
    return ((zero, zero), (zero, zero), (zero + 1.0, zero))


def widen(reach, group, other, before=None, after=None):
    is_second = (lax.axis_index("slab") & reach) > 0
    group, other = unpack(group), unpack(other)
    nothing = alone_like(group[0])
    if before is None:
        before, after = pick(is_second, other, nothing), pick(is_second, nothing, other)
    else:
        before, after = unpack(before), unpack(after)
        before, after = (
            pick(is_second, join(other, before), before),
            pick(is_second, after, join(after, other)),
        )
    group = join(pick(is_second, other, group), pick(is_second, group, other))
    return pack(group), pack(before), pack(after)


def close(reach, contact, group, before=None, after=None):
    is_upper = (lax.axis_index("slab") & reach) > 0
    group = unpack(group)
    nothing = alone_like(group[0])
    before = nothing if before is None else unpack(before)
    after = nothing if after is None else unpack(after)
    left_end, right_end = unpack(contact)
    end = pick(is_upper, right_end, left_end)
    sent = carry(pick(is_upper, flip(group), group), end)
    outer = carry(pick(is_upper, flip(after), before), end)
    inner_run = pick(is_upper, before, flip(after))
    return pack((sent,)), pack((outer,)), pack(inner_run)


def settle(reach, contact, *runs):
    return close(2 * reach, contact, *widen(reach, *runs))


def split_valleys(mine, *arrived):
    total = mine
    for part in arrived:
        total = total + part
    valleys = mine.shape[0]
    valley = lax.axis_index("valley")
    pieces = []
    for shift in range(valleys):
        owner = lax.rem(valley + shift, valleys)
        piece = total[0]
        for other in range(1, valleys):
            piece = jnp.where(owner == other, total[other], piece)
        pieces.append(piece)
    return tuple(pieces)


def on_vmem(function, *arrays):
    def kernel(*refs):
        results = function(*(ref[...] for ref in refs[: len(arrays)]))
        for ref, result in zip(refs[len(arrays) :], results, strict=True):
            ref[...] = result

    shapes = jax.eval_shape(function, *arrays)
    vmem = pl.BlockSpec(memory_space=pltpu.VMEM)
    return pl.pallas_call(
        kernel,
        out_shape=shapes,
        in_specs=[vmem] * len(arrays),
        out_specs=jax.tree.map(lambda shape: vmem, shapes),
        compiler_params=pltpu.CompilerParams(vmem_limit_bytes=SMALL_LIMIT),
    )(*arrays)


def body(
    potential,
    mode_density,
    energy,
    hopping,
    mode_energy,
    broadening,
    self_left,
    self_right,
    occupation,
):
    slabs, width = potential.shape
    modes = mode_density.shape[1]
    groups = modes // LANES
    smem = pl.BlockSpec(memory_space=pltpu.SMEM)
    vmem = pl.BlockSpec(memory_space=pltpu.VMEM)
    hbm = pl.BlockSpec(memory_space=pltpu.HBM)
    f32 = jnp.float32
    small = (potential, mode_energy, broadening, self_left, self_right)
    in_hbm = [
        pltpu.with_memory_space_constraint(array, pltpu.HBM) for array in (*small, mode_density)
    ]
    profile, onsite, contact, run = pl.pallas_call(
        project_kernel,
        out_shape=(
            jax.ShapeDtypeStruct((modes, width), mode_density.dtype),
            jax.ShapeDtypeStruct((slabs + 2, groups, LANES), f32),
            jax.ShapeDtypeStruct((4, groups, LANES), f32),
            jax.ShapeDtypeStruct((6, groups, LANES), f32),
        ),
        in_specs=[smem, smem] + [hbm] * (len(small) + 1),
        out_specs=(vmem, vmem, vmem, vmem),
        scratch_shapes=[pltpu.VMEM(array.shape, array.dtype) for array in small]
        + [
            pltpu.VMEM((groups * slabs, LANES), f32),
            pltpu.VMEM((6, groups, LANES), f32),
            pltpu.SemaphoreType.DMA((len(small),)),
            pltpu.SemaphoreType.DMA((groups,)),
        ],
        compiler_params=pltpu.CompilerParams(vmem_limit_bytes=VMEM_LIMIT),
        cost_estimate=pl.CostEstimate(
            flops=2 * slabs * width * modes, bytes_accessed=2 * width * modes, transcendentals=0
        ),
    )(energy, hopping, *in_hbm)

    count = lax.axis_size("slab")
    around = ()
    group = run
    reach = 1
    while 2 * reach < count:
        other = lax.ppermute(group, "slab", [(k, k ^ reach) for k in range(count)])
        if 4 * reach < count:
            group, *around = on_vmem(functools.partial(widen, reach), group, other, *around)
        else:
            sent, outer, inner_run = on_vmem(
                functools.partial(settle, reach), contact, group, other, *around
            )
        reach *= 2
    if count <= 2:
        sent, outer, inner_run = on_vmem(functools.partial(close, reach), contact, group)
    if count > 1:
        sent = lax.ppermute(sent, "slab", [(k, k ^ reach) for k in range(count)])
    else:
        sent = contact[2:]

    valleys, blocks = lax.axis_size("valley"), lax.axis_size("blk")
    piece = width // (valleys * blocks)
    charge, *terms = pl.pallas_call(
        functools.partial(charge_kernel, reach),
        out_shape=[jax.ShapeDtypeStruct((1, slabs, modes), f32)]
        + [jax.ShapeDtypeStruct((valleys, slabs, piece), f32)] * blocks,
        in_specs=[smem] + [vmem] * 5,
        out_specs=[hbm] + [vmem] * blocks,
        scratch_shapes=[
            pltpu.VMEM((groups * slabs, LANES), f32),
            pltpu.VMEM((1, slabs, modes), f32),
            pltpu.VMEM((slabs, modes), jnp.bfloat16),
            pltpu.SemaphoreType.DMA,
        ],
        compiler_params=pltpu.CompilerParams(vmem_limit_bytes=VMEM_LIMIT),
        cost_estimate=pl.CostEstimate(
            flops=2 * slabs * width * modes, bytes_accessed=2 * width * modes, transcendentals=0
        ),
    )(occupation, onsite, outer, inner_run, sent, profile)

    arrived = [
        lax.ppermute(terms[shift], "blk", [(k, (k + shift) % blocks) for k in range(blocks)])
        for shift in range(1, blocks)
    ]
    density, *away = on_vmem(split_valleys, terms[0], *arrived)
    for shift in range(1, valleys):
        pairs = [(k, (k + shift) % valleys) for k in range(valleys)]
        density = density + lax.ppermute(away[shift - 1], "valley", pairs)
    return charge, density


def solution(mesh):
    placed = (
        P("slab", None),
        P(("parts", "valley"), "blk", None),
        P(("parts", "valley")),
        P(("parts", "valley")),
        P(("parts", "valley"), "blk"),
        P(("parts", "valley"), "blk"),
        P(("parts", "valley"), None, "blk"),
        P(("parts", "valley"), None, "blk"),
        P(("parts", "valley")),
    )
    return jax.shard_map(
        body,
        mesh=mesh,
        in_specs=placed,
        out_specs=(P(("parts", "valley"), "slab", "blk"), P(("parts", "slab"), ("valley", "blk"))),
        check_vma=False,
    )
```

```python
import functools
import math

import jax
import jax.numpy as jnp
from jax import lax
from jax.experimental import pallas as pl
from jax.experimental.pallas import tpu as pltpu
from jax.sharding import PartitionSpec as P

LANES = 128
VMEM_LIMIT = 24 * 1024 * 1024
SMALL_LIMIT = 8 * 1024 * 1024


def times(first, second):
    return (
        first[0] * second[0] - first[1] * second[1],
        first[0] * second[1] + first[1] * second[0],
    )


def plus(first, second):
    return first[0] + second[0], first[1] + second[1]


def minus(first, second):
    return first[0] - second[0], first[1] - second[1]


def invert(value):
    scale = 1.0 / (value[0] * value[0] + value[1] * value[1])
    return value[0] * scale, -(value[1] * scale)


def one_minus(value):
    return 1.0 - value[0], -value[1]


def extend(run, slab):
    low, high, through = run
    grown = invert(minus(slab, high))
    return (
        plus(low, times(through, grown)),
        grown,
        times(through, times(grown, grown)),
    )


def join(first, second):
    low1, high1, through1 = first
    low2, high2, through2 = second
    bridge = invert(one_minus(times(high1, low2)))
    return (
        plus(low1, times(times(through1, low2), bridge)),
        plus(high2, times(times(through2, high1), bridge)),
        times(times(through1, through2), times(bridge, bridge)),
    )


def flip(run):
    return run[1], run[0], run[2]


def carry(run, value):
    low, high, through = run
    return plus(high, times(times(through, value), invert(one_minus(times(low, value)))))


def pick(flag, chosen, otherwise):
    return jax.tree.map(lambda a, b: jnp.where(flag, a, b), chosen, otherwise)


def pack(run):
    return jnp.stack([part for pair in run for part in pair])


def unpack(stack):
    return tuple((stack[2 * k], stack[2 * k + 1]) for k in range(stack.shape[0] // 2))


def fold_row(row, fold):
    for group in range(fold.shape[0]):
        fold[group : group + 1, :] = row[:, group * LANES : (group + 1) * LANES]
    return fold[...]


def scalar_kernel(energy, hopping, level_out):
    level_out[0] = jnp.full(level_out.shape[1:], energy[0], jnp.float32)
    level_out[1] = 1.0 / jnp.full(level_out.shape[1:], hopping[0], jnp.float32)


def project_kernel(
    level_in,
    potential,
    mode_energy,
    broadening,
    self_left,
    self_right,
    profile,
    onsite_out,
    contact_out,
    run_out,
    staged,
    fold,
):
    slabs = potential.shape[0]
    modes = profile.shape[1]
    groups = modes // LANES
    inverse = level_in[1]
    level = (level_in[0] - fold_row(mode_energy, fold.at[0])) * inverse
    damping = fold_row(broadening, fold.at[1]) * inverse
    for part in range(2):
        contact_out[part] = fold_row(self_left.at[0, part : part + 1], fold.at[2 + part]) * inverse
        contact_out[2 + part] = (
            fold_row(self_right.at[0, part : part + 1], fold.at[4 + part]) * inverse
        )
    onsite_out[slabs] = damping
    onsite_out[slabs + 1] = inverse
    chunk = math.gcd(modes, 256)
    for start in range(0, modes, chunk):
        result = lax.dot_general(
            potential[...],
            profile[0, start : start + chunk, :],
            (((1,), (1,)), ((), ())),
            preferred_element_type=jnp.float32,
        )
        for column in range(0, chunk, LANES):
            group = (start + column) // LANES
            staged[group * slabs : (group + 1) * slabs, :] = result[:, column : column + LANES]
    runs = []
    length = math.gcd(slabs, 4)
    for start in range(0, slabs, length):
        run = None
        for slab in range(start, start + length):
            real = level - staged[pl.ds(slab, groups, stride=slabs), :] * inverse
            onsite_out[slab] = real
            onsite = (real, damping)
            if run is None:
                alone = invert(onsite)
                run = (alone, alone, times(alone, alone))
            else:
                run = extend(run, onsite)
        runs.append(run)
    while len(runs) > 1:
        paired = [join(runs[k], runs[k + 1]) for k in range(0, len(runs) - 1, 2)]
        runs = paired + runs[2 * len(paired) :]
    for place, part in enumerate(part for pair in runs[0] for part in pair):
        run_out[place] = part


def multiply(half, profile, term, valleys, blocks, valley_shifts, block_shift):
    piece = term.shape[2]
    owner_block = lax.rem(lax.axis_index("blk") + block_shift, blocks)
    for place, shift in enumerate(valley_shifts):
        owner_valley = lax.rem(lax.axis_index("valley") + shift, valleys)
        start = pl.multiple_of((owner_valley * blocks + owner_block) * piece, piece)
        term[place] = jnp.dot(
            half[...], profile[0, :, pl.ds(start, piece)], preferred_element_type=jnp.float32
        )


def charge_kernel(
    reach,
    plan,
    occupation,
    onsite_in,
    outer_in,
    inner_run,
    sent_in,
    profile,
    charge,
    half,
    *rest,
):
    terms, staged = rest[:-1], rest[-1]
    slabs = charge.shape[1]
    groups = onsite_in.shape[1]
    outer = (outer_in[0], outer_in[1])
    inner = carry(
        tuple((inner_run[2 * k], inner_run[2 * k + 1]) for k in range(3)), (sent_in[0], sent_in[1])
    )
    is_upper = (lax.axis_index("slab") & reach) > 0
    left = pick(is_upper, inner, outer)
    right = pick(is_upper, outer, inner)
    damping = onsite_in[slabs]
    weight = (occupation[0] / math.pi) * onsite_in[slabs + 1]
    lefts, rights = [left], [right]
    for slab in range(slabs - 1):
        lefts.append(invert(minus((onsite_in[slab], damping), lefts[-1])))
        rights.append(invert(minus((onsite_in[slabs - 1 - slab], damping), rights[-1])))
    for slab in range(slabs):
        below = minus((onsite_in[slab], damping), plus(lefts[slab], rights[slabs - 1 - slab]))
        staged[pl.ds(slab, groups, stride=slabs), :] = (
            weight * below[1] / (below[0] * below[0] + below[1] * below[1])
        )
    for group in range(groups):
        columns = slice(group * LANES, (group + 1) * LANES)
        rows = staged[group * slabs : (group + 1) * slabs, :]
        charge[0, :, columns] = rows
        half[:, columns] = rows.astype(jnp.bfloat16)
    for term, block_shift in zip(terms, range(1, plan[1]), strict=True):
        multiply(half, profile, term, *plan, block_shift)


def term_kernel(plan, block_shifts, half, profile, *rest):
    for term, block_shift in zip(rest[-len(block_shifts) :], block_shifts, strict=True):
        multiply(half, profile, term, *plan, block_shift)


def store_kernel(plan, half, profile, charge, after, term, charge_hbm, leaving):
    copy = pltpu.make_async_copy(charge, charge_hbm, leaving)
    copy.start()
    multiply(half, profile, term, *plan, 0)
    copy.wait()


def alone_like(run):
    zero = jnp.zeros_like(run[0])
    return ((zero, zero), (zero, zero), (zero + 1.0, zero))


def widen(reach, group, other, before=None, after=None):
    is_second = (lax.axis_index("slab") & reach) > 0
    group, other = unpack(group), unpack(other)
    nothing = alone_like(group[0])
    if before is None:
        before, after = pick(is_second, other, nothing), pick(is_second, nothing, other)
    else:
        before, after = unpack(before), unpack(after)
        before, after = (
            pick(is_second, join(other, before), before),
            pick(is_second, after, join(after, other)),
        )
    group = join(pick(is_second, other, group), pick(is_second, group, other))
    return pack(group), pack(before), pack(after)


def close(reach, contact, group, before=None, after=None):
    is_upper = (lax.axis_index("slab") & reach) > 0
    group = unpack(group)
    nothing = alone_like(group[0])
    before = nothing if before is None else unpack(before)
    after = nothing if after is None else unpack(after)
    left_end, right_end = unpack(contact)
    end = pick(is_upper, right_end, left_end)
    sent = carry(pick(is_upper, flip(group), group), end)
    outer = carry(pick(is_upper, flip(after), before), end)
    inner_run = pick(is_upper, before, flip(after))
    return pack((sent,)), pack((outer,)), pack(inner_run)


def settle(reach, contact, *runs):
    return close(2 * reach, contact, *widen(reach, *runs))


def add_blocks(mine, *arrived):
    total = mine
    for part in arrived:
        total = total + part
    return tuple(total[place] for place in range(mine.shape[0]))


def on_vmem(function, *arrays):
    def kernel(*refs):
        results = function(*(ref[...] for ref in refs[: len(arrays)]))
        for ref, result in zip(refs[len(arrays) :], results, strict=True):
            ref[...] = result

    shapes = jax.eval_shape(function, *arrays)
    vmem = pl.BlockSpec(memory_space=pltpu.VMEM)
    return pl.pallas_call(
        kernel,
        out_shape=shapes,
        in_specs=[vmem] * len(arrays),
        out_specs=jax.tree.map(lambda shape: vmem, shapes),
        compiler_params=pltpu.CompilerParams(vmem_limit_bytes=SMALL_LIMIT),
    )(*arrays)


def body(
    potential,
    mode_density,
    energy,
    hopping,
    mode_energy,
    broadening,
    self_left,
    self_right,
    occupation,
):
    slabs, width = potential.shape
    modes = mode_density.shape[1]
    groups = modes // LANES
    smem = pl.BlockSpec(memory_space=pltpu.SMEM)
    vmem = pl.BlockSpec(memory_space=pltpu.VMEM)
    anywhere = pl.BlockSpec(memory_space=pl.ANY)
    f32 = jnp.float32
    level = pl.pallas_call(
        scalar_kernel,
        out_shape=jax.ShapeDtypeStruct((2, groups, LANES), f32),
        in_specs=[smem, smem],
        out_specs=vmem,
        compiler_params=pltpu.CompilerParams(vmem_limit_bytes=SMALL_LIMIT),
        cost_estimate=pl.CostEstimate(
            flops=600 * width * modes, bytes_accessed=8, transcendentals=0
        ),
    )(energy, hopping)
    onsite, contact, run = pl.pallas_call(
        project_kernel,
        out_shape=(
            jax.ShapeDtypeStruct((slabs + 2, groups, LANES), f32),
            jax.ShapeDtypeStruct((4, groups, LANES), f32),
            jax.ShapeDtypeStruct((6, groups, LANES), f32),
        ),
        in_specs=[vmem] * 7,
        out_specs=(vmem, vmem, vmem),
        scratch_shapes=[
            pltpu.VMEM((groups * slabs, LANES), f32),
            pltpu.VMEM((6, groups, LANES), f32),
        ],
        compiler_params=pltpu.CompilerParams(vmem_limit_bytes=VMEM_LIMIT),
        cost_estimate=pl.CostEstimate(
            flops=2 * slabs * width * modes, bytes_accessed=2 * width * modes, transcendentals=0
        ),
    )(level, potential, mode_energy, broadening, self_left, self_right, mode_density)

    count = lax.axis_size("slab")
    around = ()
    group = run
    reach = 1
    while 2 * reach < count:
        other = lax.ppermute(group, "slab", [(k, k ^ reach) for k in range(count)])
        if 4 * reach < count:
            group, *around = on_vmem(functools.partial(widen, reach), group, other, *around)
        else:
            sent, outer, inner_run = on_vmem(
                functools.partial(settle, reach), contact, group, other, *around
            )
        reach *= 2
    if count <= 2:
        sent, outer, inner_run = on_vmem(functools.partial(close, reach), contact, group)
    if count > 1:
        sent = lax.ppermute(sent, "slab", [(k, k ^ reach) for k in range(count)])
    else:
        sent = contact[2:]

    valleys, blocks = lax.axis_size("valley"), lax.axis_size("blk")
    piece = width // (valleys * blocks)
    away_plan = (valleys, blocks, tuple(range(1, valleys)))
    home_plan = (valleys, blocks, (0,))

    def term_shapes(plan, count):
        return [jax.ShapeDtypeStruct((len(plan[2]), slabs, piece), f32)] * count

    def cost(plan, count):
        columns = len(plan[2]) * count * piece
        return pl.CostEstimate(
            flops=2 * slabs * columns * modes, bytes_accessed=2 * columns * modes, transcendentals=0
        )

    def swap(terms):
        return [
            lax.ppermute(term, "blk", [(k, (k + shift) % blocks) for k in range(blocks)])
            for shift, term in enumerate(terms, 1)
        ]

    first_plan = away_plan if valleys > 1 else home_plan
    charge, half, *others = pl.pallas_call(
        functools.partial(charge_kernel, reach, first_plan),
        out_shape=[
            jax.ShapeDtypeStruct((1, slabs, modes), f32),
            jax.ShapeDtypeStruct((slabs, modes), jnp.bfloat16),
        ]
        + term_shapes(first_plan, blocks - 1),
        in_specs=[smem] + [vmem] * 5,
        out_specs=[vmem] * (blocks + 1),
        scratch_shapes=[pltpu.VMEM((groups * slabs, LANES), f32)],
        compiler_params=pltpu.CompilerParams(vmem_limit_bytes=VMEM_LIMIT),
        cost_estimate=cost(first_plan, blocks - 1),
    )(occupation, onsite, outer, inner_run, sent, mode_density)

    def terms_of(plan, block_shifts, *after):
        return pl.pallas_call(
            functools.partial(term_kernel, plan, block_shifts),
            out_shape=term_shapes(plan, len(block_shifts)),
            in_specs=[vmem] * 2 + [anywhere] * len(after),
            out_specs=[vmem] * len(block_shifts),
            compiler_params=pltpu.CompilerParams(vmem_limit_bytes=VMEM_LIMIT),
            cost_estimate=cost(plan, len(block_shifts)),
        )(half, mode_density, *after)

    others = swap(others)
    arrived = []
    after = half
    if valleys > 1:
        away = on_vmem(add_blocks, *terms_of(away_plan, (0,)), *others)
        after = away[0]
        for shift in range(1, valleys):
            pairs = [(k, (k + shift) % valleys) for k in range(valleys)]
            arrived.append(lax.ppermute(away[shift - 1], "valley", pairs))
        if blocks > 1:
            others = swap(terms_of(home_plan, range(1, blocks), after))
    term, charge = pl.pallas_call(
        functools.partial(store_kernel, home_plan),
        out_shape=term_shapes(home_plan, 1) + [jax.ShapeDtypeStruct(charge.shape, f32)],
        in_specs=[vmem] * 3 + [anywhere],
        out_specs=[vmem, anywhere],
        scratch_shapes=[pltpu.SemaphoreType.DMA],
        compiler_params=pltpu.CompilerParams(vmem_limit_bytes=VMEM_LIMIT),
        cost_estimate=cost(home_plan, 1),
    )(half, mode_density, charge, after)
    density = term[0]
    for part in others:
        density = density + part[0]
    for part in arrived:
        density = density + part
    return charge, density


def solution(mesh):
    placed = (
        P("slab", None),
        P(("parts", "valley"), "blk", None),
        P(("parts", "valley")),
        P(("parts", "valley")),
        P(("parts", "valley"), "blk"),
        P(("parts", "valley"), "blk"),
        P(("parts", "valley"), None, "blk"),
        P(("parts", "valley"), None, "blk"),
        P(("parts", "valley")),
    )
    return jax.shard_map(
        body,
        mesh=mesh,
        in_specs=placed,
        out_specs=(P(("parts", "valley"), "slab", "blk"), P(("parts", "slab"), ("valley", "blk"))),
        check_vma=False,
    )
```

```python
import functools
import math

import jax
import jax.numpy as jnp
from jax import lax
from jax.experimental import pallas as pl
from jax.experimental.pallas import tpu as pltpu
from jax.sharding import PartitionSpec as P

LANES = 128
VMEM_LIMIT = 24 * 1024 * 1024
SMALL_LIMIT = 8 * 1024 * 1024


def times(first, second):
    return (
        first[0] * second[0] - first[1] * second[1],
        first[0] * second[1] + first[1] * second[0],
    )


def plus(first, second):
    return first[0] + second[0], first[1] + second[1]


def minus(first, second):
    return first[0] - second[0], first[1] - second[1]


def invert(value):
    scale = 1.0 / (value[0] * value[0] + value[1] * value[1])
    return value[0] * scale, -(value[1] * scale)


def one_minus(value):
    return 1.0 - value[0], -value[1]


def extend(run, slab):
    low, high, through = run
    grown = invert(minus(slab, high))
    return (
        plus(low, times(through, grown)),
        grown,
        times(through, times(grown, grown)),
    )


def join(first, second):
    low1, high1, through1 = first
    low2, high2, through2 = second
    bridge = invert(one_minus(times(high1, low2)))
    return (
        plus(low1, times(times(through1, low2), bridge)),
        plus(high2, times(times(through2, high1), bridge)),
        times(times(through1, through2), times(bridge, bridge)),
    )


def flip(run):
    return run[1], run[0], run[2]


def carry(run, value):
    low, high, through = run
    return plus(high, times(times(through, value), invert(one_minus(times(low, value)))))


def pick(flag, chosen, otherwise):
    return jax.tree.map(lambda a, b: jnp.where(flag, a, b), chosen, otherwise)


def pack(run):
    return jnp.stack([part for pair in run for part in pair])


def unpack(stack):
    return tuple((stack[2 * k], stack[2 * k + 1]) for k in range(stack.shape[0] // 2))


def fold_row(row, fold):
    for group in range(fold.shape[0]):
        fold[group : group + 1, :] = row[:, group * LANES : (group + 1) * LANES]
    return fold[...]


def contract(first, second):
    return lax.dot_general(
        first, second, (((1,), (1,)), ((), ())), preferred_element_type=jnp.float32
    )


def scalar_kernel(energy, hopping, level_out):
    level_out[0] = jnp.full(level_out.shape[1:], energy[0], jnp.float32)
    level_out[1] = 1.0 / jnp.full(level_out.shape[1:], hopping[0], jnp.float32)


def project_kernel(
    level_in,
    potential,
    mode_energy,
    broadening,
    self_left,
    self_right,
    profile,
    onsite_out,
    contact_out,
    run_out,
    staged,
    fold,
):
    slabs = potential.shape[0]
    groups = run_out.shape[1]
    inverse = level_in[1]
    level = (level_in[0] - fold_row(mode_energy, fold.at[0])) * inverse
    damping = fold_row(broadening, fold.at[1]) * inverse
    for part in range(2):
        contact_out[part] = fold_row(self_left.at[0, part : part + 1], fold.at[2 + part]) * inverse
        contact_out[2 + part] = (
            fold_row(self_right.at[0, part : part + 1], fold.at[4 + part]) * inverse
        )
    onsite_out[slabs] = damping
    onsite_out[slabs + 1] = inverse
    split = groups // 2 * LANES
    width = profile.shape[2]
    depth = math.gcd(width, 256)
    first, second = [], []
    for start in range(0, width, depth):
        points = slice(start, start + depth)
        if split:
            first.append(contract(potential[:, points], profile[0, :split, points]))
        second.append(contract(profile[0, split:, points], potential[:, points]))
    result = functools.reduce(jnp.add, second).T
    if split:
        result = jnp.concatenate([functools.reduce(jnp.add, first), result], axis=1)
    for group in range(groups):
        staged[group * slabs : (group + 1) * slabs, :] = result[
            :, group * LANES : (group + 1) * LANES
        ]
    runs = []
    length = math.gcd(slabs, 4)
    for start in range(0, slabs, length):
        run = None
        for slab in range(start, start + length):
            real = level - staged[pl.ds(slab, groups, stride=slabs), :] * inverse
            onsite_out[slab] = real
            onsite = (real, damping)
            if run is None:
                alone = invert(onsite)
                run = (alone, alone, times(alone, alone))
            else:
                run = extend(run, onsite)
        runs.append(run)
    while len(runs) > 1:
        paired = [join(runs[k], runs[k + 1]) for k in range(0, len(runs) - 1, 2)]
        runs = paired + runs[2 * len(paired) :]
    for place, part in enumerate(part for pair in runs[0] for part in pair):
        run_out[place] = part


def multiply(half, profile, term, valleys, blocks, valley_shifts, block_shift):
    piece = term.shape[2]
    owner_block = lax.rem(lax.axis_index("blk") + block_shift, blocks)
    for place, shift in enumerate(valley_shifts):
        owner_valley = lax.rem(lax.axis_index("valley") + shift, valleys)
        start = pl.multiple_of((owner_valley * blocks + owner_block) * piece, piece)
        term[place] = jnp.dot(
            half[...], profile[0, :, pl.ds(start, piece)], preferred_element_type=jnp.float32
        )


def charge_kernel(
    reach,
    plan,
    occupation,
    onsite_in,
    outer_in,
    inner_run,
    sent_in,
    profile,
    charge,
    half,
    *rest,
):
    terms, staged = rest[:-1], rest[-1]
    slabs = charge.shape[1]
    groups = onsite_in.shape[1]
    outer = (outer_in[0], outer_in[1])
    inner = carry(
        tuple((inner_run[2 * k], inner_run[2 * k + 1]) for k in range(3)), (sent_in[0], sent_in[1])
    )
    is_upper = (lax.axis_index("slab") & reach) > 0
    left = pick(is_upper, inner, outer)
    right = pick(is_upper, outer, inner)
    damping = onsite_in[slabs]
    weight = (occupation[0] / math.pi) * onsite_in[slabs + 1]
    lefts, rights = [left], [right]
    for slab in range(slabs - 1):
        lefts.append(invert(minus((onsite_in[slab], damping), lefts[-1])))
        rights.append(invert(minus((onsite_in[slabs - 1 - slab], damping), rights[-1])))
    for slab in range(slabs):
        below = minus((onsite_in[slab], damping), plus(lefts[slab], rights[slabs - 1 - slab]))
        staged[pl.ds(slab, groups, stride=slabs), :] = (
            weight * below[1] / (below[0] * below[0] + below[1] * below[1])
        )
    for group in range(groups):
        columns = slice(group * LANES, (group + 1) * LANES)
        rows = staged[group * slabs : (group + 1) * slabs, :]
        charge[0, :, columns] = rows
        half[:, columns] = rows.astype(jnp.bfloat16)
    for term, block_shift in zip(terms, range(1, plan[1]), strict=True):
        multiply(half, profile, term, *plan, block_shift)


def term_kernel(plan, block_shifts, half, profile, *rest):
    for term, block_shift in zip(rest[-len(block_shifts) :], block_shifts, strict=True):
        multiply(half, profile, term, *plan, block_shift)


def store_kernel(plan, half, profile, charge, after, term, charge_hbm, leaving):
    copy = pltpu.make_async_copy(charge, charge_hbm, leaving)
    copy.start()
    multiply(half, profile, term, *plan, 0)
    copy.wait()


def alone_like(run):
    zero = jnp.zeros_like(run[0])
    return ((zero, zero), (zero, zero), (zero + 1.0, zero))


def widen(reach, group, other, before=None, after=None):
    is_second = (lax.axis_index("slab") & reach) > 0
    group, other = unpack(group), unpack(other)
    nothing = alone_like(group[0])
    if before is None:
        before, after = pick(is_second, other, nothing), pick(is_second, nothing, other)
    else:
        before, after = unpack(before), unpack(after)
        before, after = (
            pick(is_second, join(other, before), before),
            pick(is_second, after, join(after, other)),
        )
    group = join(pick(is_second, other, group), pick(is_second, group, other))
    return pack(group), pack(before), pack(after)


def close(reach, contact, group, before=None, after=None):
    is_upper = (lax.axis_index("slab") & reach) > 0
    group = unpack(group)
    nothing = alone_like(group[0])
    before = nothing if before is None else unpack(before)
    after = nothing if after is None else unpack(after)
    left_end, right_end = unpack(contact)
    end = pick(is_upper, right_end, left_end)
    sent = carry(pick(is_upper, flip(group), group), end)
    outer = carry(pick(is_upper, flip(after), before), end)
    inner_run = pick(is_upper, before, flip(after))
    return pack((sent,)), pack((outer,)), pack(inner_run)


def settle(reach, contact, *runs):
    return close(2 * reach, contact, *widen(reach, *runs))


def add_blocks(mine, *arrived):
    total = mine
    for part in arrived:
        total = total + part
    return tuple(total[place] for place in range(mine.shape[0]))


def on_vmem(function, *arrays):
    def kernel(*refs):
        results = function(*(ref[...] for ref in refs[: len(arrays)]))
        for ref, result in zip(refs[len(arrays) :], results, strict=True):
            ref[...] = result

    shapes = jax.eval_shape(function, *arrays)
    vmem = pl.BlockSpec(memory_space=pltpu.VMEM)
    return pl.pallas_call(
        kernel,
        out_shape=shapes,
        in_specs=[vmem] * len(arrays),
        out_specs=jax.tree.map(lambda shape: vmem, shapes),
        compiler_params=pltpu.CompilerParams(vmem_limit_bytes=SMALL_LIMIT),
    )(*arrays)


def body(
    potential,
    mode_density,
    energy,
    hopping,
    mode_energy,
    broadening,
    self_left,
    self_right,
    occupation,
):
    slabs, width = potential.shape
    modes = mode_density.shape[1]
    groups = modes // LANES
    smem = pl.BlockSpec(memory_space=pltpu.SMEM)
    vmem = pl.BlockSpec(memory_space=pltpu.VMEM)
    anywhere = pl.BlockSpec(memory_space=pl.ANY)
    f32 = jnp.float32
    level = pl.pallas_call(
        scalar_kernel,
        out_shape=jax.ShapeDtypeStruct((2, groups, LANES), f32),
        in_specs=[smem, smem],
        out_specs=vmem,
        compiler_params=pltpu.CompilerParams(vmem_limit_bytes=SMALL_LIMIT),
        cost_estimate=pl.CostEstimate(
            flops=600 * width * modes, bytes_accessed=8, transcendentals=0
        ),
    )(energy, hopping)
    onsite, contact, run = pl.pallas_call(
        project_kernel,
        out_shape=(
            jax.ShapeDtypeStruct((slabs + 2, groups, LANES), f32),
            jax.ShapeDtypeStruct((4, groups, LANES), f32),
            jax.ShapeDtypeStruct((6, groups, LANES), f32),
        ),
        in_specs=[vmem] * 7,
        out_specs=(vmem, vmem, vmem),
        scratch_shapes=[
            pltpu.VMEM((groups * slabs, LANES), f32),
            pltpu.VMEM((6, groups, LANES), f32),
        ],
        compiler_params=pltpu.CompilerParams(vmem_limit_bytes=VMEM_LIMIT),
        cost_estimate=pl.CostEstimate(
            flops=2 * slabs * width * modes, bytes_accessed=2 * width * modes, transcendentals=0
        ),
    )(level, potential, mode_energy, broadening, self_left, self_right, mode_density)

    count = lax.axis_size("slab")
    around = ()
    group = run
    reach = 1
    while 2 * reach < count:
        other = lax.ppermute(group, "slab", [(k, k ^ reach) for k in range(count)])
        if 4 * reach < count:
            group, *around = on_vmem(functools.partial(widen, reach), group, other, *around)
        else:
            sent, outer, inner_run = on_vmem(
                functools.partial(settle, reach), contact, group, other, *around
            )
        reach *= 2
    if count <= 2:
        sent, outer, inner_run = on_vmem(functools.partial(close, reach), contact, group)
    if count > 1:
        sent = lax.ppermute(sent, "slab", [(k, k ^ reach) for k in range(count)])
    else:
        sent = contact[2:]

    valleys, blocks = lax.axis_size("valley"), lax.axis_size("blk")
    piece = width // (valleys * blocks)
    away_plan = (valleys, blocks, tuple(range(1, valleys)))
    home_plan = (valleys, blocks, (0,))

    def term_shapes(plan, count):
        return [jax.ShapeDtypeStruct((len(plan[2]), slabs, piece), f32)] * count

    def cost(plan, count):
        columns = len(plan[2]) * count * piece
        return pl.CostEstimate(
            flops=2 * slabs * columns * modes, bytes_accessed=2 * columns * modes, transcendentals=0
        )

    def swap(terms):
        return [
            lax.ppermute(term, "blk", [(k, (k + shift) % blocks) for k in range(blocks)])
            for shift, term in enumerate(terms, 1)
        ]

    first_plan = away_plan if valleys > 1 else home_plan
    charge, half, *others = pl.pallas_call(
        functools.partial(charge_kernel, reach, first_plan),
        out_shape=[
            jax.ShapeDtypeStruct((1, slabs, modes), f32),
            jax.ShapeDtypeStruct((slabs, modes), jnp.bfloat16),
        ]
        + term_shapes(first_plan, blocks - 1),
        in_specs=[smem] + [vmem] * 5,
        out_specs=[vmem] * (blocks + 1),
        scratch_shapes=[pltpu.VMEM((groups * slabs, LANES), f32)],
        compiler_params=pltpu.CompilerParams(vmem_limit_bytes=VMEM_LIMIT),
        cost_estimate=cost(first_plan, blocks - 1),
    )(occupation, onsite, outer, inner_run, sent, mode_density)

    def terms_of(plan, block_shifts, *after):
        return pl.pallas_call(
            functools.partial(term_kernel, plan, block_shifts),
            out_shape=term_shapes(plan, len(block_shifts)),
            in_specs=[vmem] * 2 + [anywhere] * len(after),
            out_specs=[vmem] * len(block_shifts),
            compiler_params=pltpu.CompilerParams(vmem_limit_bytes=VMEM_LIMIT),
            cost_estimate=cost(plan, len(block_shifts)),
        )(half, mode_density, *after)

    others = swap(others)
    arrived = []
    after = half
    if valleys > 1:
        away = on_vmem(add_blocks, *terms_of(away_plan, (0,)), *others)
        after = away[0]
        for shift in range(1, valleys):
            pairs = [(k, (k + shift) % valleys) for k in range(valleys)]
            arrived.append(lax.ppermute(away[shift - 1], "valley", pairs))
        if blocks > 1:
            others = swap(terms_of(home_plan, range(1, blocks), after))
    term, charge = pl.pallas_call(
        functools.partial(store_kernel, home_plan),
        out_shape=term_shapes(home_plan, 1) + [jax.ShapeDtypeStruct(charge.shape, f32)],
        in_specs=[vmem] * 3 + [anywhere],
        out_specs=[vmem, anywhere],
        scratch_shapes=[pltpu.SemaphoreType.DMA],
        compiler_params=pltpu.CompilerParams(vmem_limit_bytes=VMEM_LIMIT),
        cost_estimate=cost(home_plan, 1),
    )(half, mode_density, charge, after)
    density = term[0]
    for part in others:
        density = density + part[0]
    for part in arrived:
        density = density + part
    return charge, density


def solution(mesh):
    placed = (
        P("slab", None),
        P(("parts", "valley"), "blk", None),
        P(("parts", "valley")),
        P(("parts", "valley")),
        P(("parts", "valley"), "blk"),
        P(("parts", "valley"), "blk"),
        P(("parts", "valley"), None, "blk"),
        P(("parts", "valley"), None, "blk"),
        P(("parts", "valley")),
    )
    return jax.shard_map(
        body,
        mesh=mesh,
        in_specs=placed,
        out_specs=(P(("parts", "valley"), "slab", "blk"), P(("parts", "slab"), ("valley", "blk"))),
        check_vma=False,
    )
```

```python
import functools
import math

import jax
import jax.numpy as jnp
from jax import lax
from jax.experimental import pallas as pl
from jax.experimental.pallas import tpu as pltpu
from jax.sharding import PartitionSpec as P

LANES = 128
VMEM_LIMIT = 24 * 1024 * 1024
SMALL_LIMIT = 8 * 1024 * 1024


def times(first, second):
    return (
        first[0] * second[0] - first[1] * second[1],
        first[0] * second[1] + first[1] * second[0],
    )


def plus(first, second):
    return first[0] + second[0], first[1] + second[1]


def minus(first, second):
    return first[0] - second[0], first[1] - second[1]


def invert(value):
    scale = 1.0 / (value[0] * value[0] + value[1] * value[1])
    return value[0] * scale, -(value[1] * scale)


def one_minus(value):
    return 1.0 - value[0], -value[1]


def extend(run, slab):
    low, high, through = run
    grown = invert(minus(slab, high))
    return (
        plus(low, times(through, grown)),
        grown,
        times(through, times(grown, grown)),
    )


def join(first, second):
    low1, high1, through1 = first
    low2, high2, through2 = second
    bridge = invert(one_minus(times(high1, low2)))
    return (
        plus(low1, times(times(through1, low2), bridge)),
        plus(high2, times(times(through2, high1), bridge)),
        times(times(through1, through2), times(bridge, bridge)),
    )


def flip(run):
    return run[1], run[0], run[2]


def carry(run, value):
    low, high, through = run
    return plus(high, times(times(through, value), invert(one_minus(times(low, value)))))


def pick(flag, chosen, otherwise):
    return jax.tree.map(lambda a, b: jnp.where(flag, a, b), chosen, otherwise)


def pack(run):
    return jnp.stack([part for pair in run for part in pair])


def unpack(stack):
    return tuple((stack[2 * k], stack[2 * k + 1]) for k in range(stack.shape[0] // 2))


def fold_row(row, fold):
    for group in range(fold.shape[0]):
        fold[group : group + 1, :] = row[:, group * LANES : (group + 1) * LANES]
    return fold[...]


def contract(first, second):
    return lax.dot_general(
        first, second, (((1,), (1,)), ((), ())), preferred_element_type=jnp.float32
    )


def scalar_kernel(energy, hopping, level_out):
    level_out[0] = jnp.full(level_out.shape[1:], energy[0], jnp.float32)
    level_out[1] = 1.0 / jnp.full(level_out.shape[1:], hopping[0], jnp.float32)


def project_kernel(
    level_in,
    potential,
    mode_energy,
    broadening,
    self_left,
    self_right,
    profile,
    onsite_out,
    contact_out,
    run_out,
    staged,
    fold,
):
    slabs = potential.shape[0]
    groups = run_out.shape[1]
    inverse = level_in[1]
    level = (level_in[0] - fold_row(mode_energy, fold.at[0])) * inverse
    damping = fold_row(broadening, fold.at[1]) * inverse
    for part in range(2):
        contact_out[part] = fold_row(self_left.at[0, part : part + 1], fold.at[2 + part]) * inverse
        contact_out[2 + part] = (
            fold_row(self_right.at[0, part : part + 1], fold.at[4 + part]) * inverse
        )
    onsite_out[slabs] = damping
    onsite_out[slabs + 1] = inverse
    width = profile.shape[2]
    depth = math.gcd(width, 256)
    block = math.gcd(groups, 2) * LANES
    totals = [None] * (groups * LANES // block)
    for start in range(0, width, depth):
        points = slice(start, start + depth)
        for place, total in enumerate(totals):
            rows = profile[0, place * block : (place + 1) * block, points]
            if place % 2:
                term = contract(rows, potential[:, points])
            else:
                term = contract(potential[:, points], rows)
            totals[place] = term if total is None else total + term
    for place, total in enumerate(totals):
        result = total.T if place % 2 else total
        for column in range(0, block, LANES):
            group = (place * block + column) // LANES
            staged[group * slabs : (group + 1) * slabs, :] = result[:, column : column + LANES]
    runs = []
    length = math.gcd(slabs, 4)
    for start in range(0, slabs, length):
        run = None
        for slab in range(start, start + length):
            real = level - staged[pl.ds(slab, groups, stride=slabs), :] * inverse
            onsite_out[slab] = real
            onsite = (real, damping)
            if run is None:
                alone = invert(onsite)
                run = (alone, alone, times(alone, alone))
            else:
                run = extend(run, onsite)
        runs.append(run)
    while len(runs) > 1:
        paired = [join(runs[k], runs[k + 1]) for k in range(0, len(runs) - 1, 2)]
        runs = paired + runs[2 * len(paired) :]
    for place, part in enumerate(part for pair in runs[0] for part in pair):
        run_out[place] = part


def multiply(half, profile, term, valleys, blocks, valley_shifts, block_shift):
    piece = term.shape[2]
    owner_block = lax.rem(lax.axis_index("blk") + block_shift, blocks)
    for place, shift in enumerate(valley_shifts):
        owner_valley = lax.rem(lax.axis_index("valley") + shift, valleys)
        start = pl.multiple_of((owner_valley * blocks + owner_block) * piece, piece)
        term[place] = jnp.dot(
            half[...], profile[0, :, pl.ds(start, piece)], preferred_element_type=jnp.float32
        )


def charge_kernel(
    reach,
    plan,
    occupation,
    onsite_in,
    outer_in,
    inner_run,
    sent_in,
    profile,
    charge,
    half,
    *rest,
):
    terms, staged = rest[:-1], rest[-1]
    slabs = charge.shape[1]
    groups = onsite_in.shape[1]
    outer = (outer_in[0], outer_in[1])
    inner = carry(
        tuple((inner_run[2 * k], inner_run[2 * k + 1]) for k in range(3)), (sent_in[0], sent_in[1])
    )
    is_upper = (lax.axis_index("slab") & reach) > 0
    left = pick(is_upper, inner, outer)
    right = pick(is_upper, outer, inner)
    damping = onsite_in[slabs]
    weight = (occupation[0] / math.pi) * onsite_in[slabs + 1]
    lefts, rights = [left], [right]
    for slab in range(slabs - 1):
        lefts.append(invert(minus((onsite_in[slab], damping), lefts[-1])))
        rights.append(invert(minus((onsite_in[slabs - 1 - slab], damping), rights[-1])))
    for slab in range(slabs):
        below = minus((onsite_in[slab], damping), plus(lefts[slab], rights[slabs - 1 - slab]))
        staged[pl.ds(slab, groups, stride=slabs), :] = (
            weight * below[1] / (below[0] * below[0] + below[1] * below[1])
        )
    for group in range(groups):
        columns = slice(group * LANES, (group + 1) * LANES)
        rows = staged[group * slabs : (group + 1) * slabs, :]
        charge[0, :, columns] = rows
        half[:, columns] = rows.astype(jnp.bfloat16)
    for term, block_shift in zip(terms, range(1, plan[1]), strict=True):
        multiply(half, profile, term, *plan, block_shift)


def term_kernel(plan, block_shifts, half, profile, *rest):
    for term, block_shift in zip(rest[-len(block_shifts) :], block_shifts, strict=True):
        multiply(half, profile, term, *plan, block_shift)


def store_kernel(plan, half, profile, charge, after, term, charge_hbm, leaving):
    copy = pltpu.make_async_copy(charge, charge_hbm, leaving)
    copy.start()
    multiply(half, profile, term, *plan, 0)
    copy.wait()


def alone_like(run):
    zero = jnp.zeros_like(run[0])
    return ((zero, zero), (zero, zero), (zero + 1.0, zero))


def widen(reach, group, other, before=None, after=None):
    is_second = (lax.axis_index("slab") & reach) > 0
    group, other = unpack(group), unpack(other)
    nothing = alone_like(group[0])
    if before is None:
        before, after = pick(is_second, other, nothing), pick(is_second, nothing, other)
    else:
        before, after = unpack(before), unpack(after)
        before, after = (
            pick(is_second, join(other, before), before),
            pick(is_second, after, join(after, other)),
        )
    group = join(pick(is_second, other, group), pick(is_second, group, other))
    return pack(group), pack(before), pack(after)


def close(reach, contact, group, before=None, after=None):
    is_upper = (lax.axis_index("slab") & reach) > 0
    group = unpack(group)
    nothing = alone_like(group[0])
    before = nothing if before is None else unpack(before)
    after = nothing if after is None else unpack(after)
    left_end, right_end = unpack(contact)
    end = pick(is_upper, right_end, left_end)
    sent = carry(pick(is_upper, flip(group), group), end)
    outer = carry(pick(is_upper, flip(after), before), end)
    inner_run = pick(is_upper, before, flip(after))
    return pack((sent,)), pack((outer,)), pack(inner_run)


def settle(reach, contact, *runs):
    return close(2 * reach, contact, *widen(reach, *runs))


def add_blocks(mine, *arrived):
    total = mine
    for part in arrived:
        total = total + part
    return tuple(total[place] for place in range(mine.shape[0]))


def on_vmem(function, *arrays):
    def kernel(*refs):
        results = function(*(ref[...] for ref in refs[: len(arrays)]))
        for ref, result in zip(refs[len(arrays) :], results, strict=True):
            ref[...] = result

    shapes = jax.eval_shape(function, *arrays)
    vmem = pl.BlockSpec(memory_space=pltpu.VMEM)
    return pl.pallas_call(
        kernel,
        out_shape=shapes,
        in_specs=[vmem] * len(arrays),
        out_specs=jax.tree.map(lambda shape: vmem, shapes),
        compiler_params=pltpu.CompilerParams(vmem_limit_bytes=SMALL_LIMIT),
    )(*arrays)


def body(
    potential,
    mode_density,
    energy,
    hopping,
    mode_energy,
    broadening,
    self_left,
    self_right,
    occupation,
):
    slabs, width = potential.shape
    modes = mode_density.shape[1]
    groups = modes // LANES
    smem = pl.BlockSpec(memory_space=pltpu.SMEM)
    vmem = pl.BlockSpec(memory_space=pltpu.VMEM)
    anywhere = pl.BlockSpec(memory_space=pl.ANY)
    f32 = jnp.float32
    level = pl.pallas_call(
        scalar_kernel,
        out_shape=jax.ShapeDtypeStruct((2, groups, LANES), f32),
        in_specs=[smem, smem],
        out_specs=vmem,
        compiler_params=pltpu.CompilerParams(vmem_limit_bytes=SMALL_LIMIT),
        cost_estimate=pl.CostEstimate(
            flops=600 * width * modes, bytes_accessed=8, transcendentals=0
        ),
    )(energy, hopping)
    onsite, contact, run = pl.pallas_call(
        project_kernel,
        out_shape=(
            jax.ShapeDtypeStruct((slabs + 2, groups, LANES), f32),
            jax.ShapeDtypeStruct((4, groups, LANES), f32),
            jax.ShapeDtypeStruct((6, groups, LANES), f32),
        ),
        in_specs=[vmem] * 7,
        out_specs=(vmem, vmem, vmem),
        scratch_shapes=[
            pltpu.VMEM((groups * slabs, LANES), f32),
            pltpu.VMEM((6, groups, LANES), f32),
        ],
        compiler_params=pltpu.CompilerParams(vmem_limit_bytes=VMEM_LIMIT),
        cost_estimate=pl.CostEstimate(
            flops=2 * slabs * width * modes, bytes_accessed=2 * width * modes, transcendentals=0
        ),
    )(level, potential, mode_energy, broadening, self_left, self_right, mode_density)

    count = lax.axis_size("slab")
    around = ()
    group = run
    reach = 1
    while 2 * reach < count:
        other = lax.ppermute(group, "slab", [(k, k ^ reach) for k in range(count)])
        if 4 * reach < count:
            group, *around = on_vmem(functools.partial(widen, reach), group, other, *around)
        else:
            sent, outer, inner_run = on_vmem(
                functools.partial(settle, reach), contact, group, other, *around
            )
        reach *= 2
    if count <= 2:
        sent, outer, inner_run = on_vmem(functools.partial(close, reach), contact, group)
    if count > 1:
        sent = lax.ppermute(sent, "slab", [(k, k ^ reach) for k in range(count)])
    else:
        sent = contact[2:]

    valleys, blocks = lax.axis_size("valley"), lax.axis_size("blk")
    piece = width // (valleys * blocks)
    away_plan = (valleys, blocks, tuple(range(1, valleys)))
    home_plan = (valleys, blocks, (0,))

    def term_shapes(plan, count):
        return [jax.ShapeDtypeStruct((len(plan[2]), slabs, piece), f32)] * count

    def cost(plan, count):
        columns = len(plan[2]) * count * piece
        return pl.CostEstimate(
            flops=2 * slabs * columns * modes, bytes_accessed=2 * columns * modes, transcendentals=0
        )

    def swap(terms):
        return [
            lax.ppermute(term, "blk", [(k, (k + shift) % blocks) for k in range(blocks)])
            for shift, term in enumerate(terms, 1)
        ]

    first_plan = away_plan if valleys > 1 else home_plan
    charge, half, *others = pl.pallas_call(
        functools.partial(charge_kernel, reach, first_plan),
        out_shape=[
            jax.ShapeDtypeStruct((1, slabs, modes), f32),
            jax.ShapeDtypeStruct((slabs, modes), jnp.bfloat16),
        ]
        + term_shapes(first_plan, blocks - 1),
        in_specs=[smem] + [vmem] * 5,
        out_specs=[vmem] * (blocks + 1),
        scratch_shapes=[pltpu.VMEM((groups * slabs, LANES), f32)],
        compiler_params=pltpu.CompilerParams(vmem_limit_bytes=VMEM_LIMIT),
        cost_estimate=cost(first_plan, blocks - 1),
    )(occupation, onsite, outer, inner_run, sent, mode_density)

    def terms_of(plan, block_shifts, *after):
        return pl.pallas_call(
            functools.partial(term_kernel, plan, block_shifts),
            out_shape=term_shapes(plan, len(block_shifts)),
            in_specs=[vmem] * 2 + [anywhere] * len(after),
            out_specs=[vmem] * len(block_shifts),
            compiler_params=pltpu.CompilerParams(vmem_limit_bytes=VMEM_LIMIT),
            cost_estimate=cost(plan, len(block_shifts)),
        )(half, mode_density, *after)

    others = swap(others)
    arrived = []
    after = half
    if valleys > 1:
        away = on_vmem(add_blocks, *terms_of(away_plan, (0,)), *others)
        after = away[0]
        for shift in range(1, valleys):
            pairs = [(k, (k + shift) % valleys) for k in range(valleys)]
            arrived.append(lax.ppermute(away[shift - 1], "valley", pairs))
        if blocks > 1:
            others = swap(terms_of(home_plan, range(1, blocks), after))
    term, charge = pl.pallas_call(
        functools.partial(store_kernel, home_plan),
        out_shape=term_shapes(home_plan, 1) + [jax.ShapeDtypeStruct(charge.shape, f32)],
        in_specs=[vmem] * 3 + [anywhere],
        out_specs=[vmem, anywhere],
        scratch_shapes=[pltpu.SemaphoreType.DMA],
        compiler_params=pltpu.CompilerParams(vmem_limit_bytes=VMEM_LIMIT),
        cost_estimate=cost(home_plan, 1),
    )(half, mode_density, charge, after)
    density = term[0]
    for part in others:
        density = density + part[0]
    for part in arrived:
        density = density + part
    return charge, density


def solution(mesh):
    placed = (
        P("slab", None),
        P(("parts", "valley"), "blk", None),
        P(("parts", "valley")),
        P(("parts", "valley")),
        P(("parts", "valley"), "blk"),
        P(("parts", "valley"), "blk"),
        P(("parts", "valley"), None, "blk"),
        P(("parts", "valley"), None, "blk"),
        P(("parts", "valley")),
    )
    return jax.shard_map(
        body,
        mesh=mesh,
        in_specs=placed,
        out_specs=(P(("parts", "valley"), "slab", "blk"), P(("parts", "slab"), ("valley", "blk"))),
        check_vma=False,
    )
```

```python
import functools
import math

import jax
import jax.numpy as jnp
from jax import lax
from jax.experimental import pallas as pl
from jax.experimental.pallas import tpu as pltpu
from jax.sharding import PartitionSpec as P

LANES = 128
VMEM_LIMIT = 24 * 1024 * 1024
SMALL_LIMIT = 8 * 1024 * 1024


def times(first, second):
    return (
        first[0] * second[0] - first[1] * second[1],
        first[0] * second[1] + first[1] * second[0],
    )


def plus(first, second):
    return first[0] + second[0], first[1] + second[1]


def minus(first, second):
    return first[0] - second[0], first[1] - second[1]


def invert(value):
    scale = 1.0 / (value[0] * value[0] + value[1] * value[1])
    return value[0] * scale, -(value[1] * scale)


def one_minus(value):
    return 1.0 - value[0], -value[1]


def extend(run, slab):
    low, high, through = run
    grown = invert(minus(slab, high))
    return (
        plus(low, times(through, grown)),
        grown,
        times(through, times(grown, grown)),
    )


def join(first, second):
    low1, high1, through1 = first
    low2, high2, through2 = second
    bridge = invert(one_minus(times(high1, low2)))
    return (
        plus(low1, times(times(through1, low2), bridge)),
        plus(high2, times(times(through2, high1), bridge)),
        times(times(through1, through2), times(bridge, bridge)),
    )


def flip(run):
    return run[1], run[0], run[2]


def carry(run, value):
    low, high, through = run
    return plus(high, times(times(through, value), invert(one_minus(times(low, value)))))


def pick(flag, chosen, otherwise):
    return jax.tree.map(lambda a, b: jnp.where(flag, a, b), chosen, otherwise)


def pack(run):
    return jnp.stack([part for pair in run for part in pair])


def unpack(stack):
    return tuple((stack[2 * k], stack[2 * k + 1]) for k in range(stack.shape[0] // 2))


def fold_row(row, fold):
    for group in range(fold.shape[0]):
        fold[group : group + 1, :] = row[:, group * LANES : (group + 1) * LANES]
    return fold[...]


def contract(first, second):
    return lax.dot_general(
        first, second, (((1,), (1,)), ((), ())), preferred_element_type=jnp.float32
    )


def scalar_kernel(energy, hopping, level_out):
    level_out[0] = jnp.full(level_out.shape[1:], energy[0], jnp.float32)
    level_out[1] = 1.0 / jnp.full(level_out.shape[1:], hopping[0], jnp.float32)


def project_kernel(
    level_in,
    potential,
    mode_energy,
    broadening,
    self_left,
    self_right,
    profile,
    onsite_out,
    contact_out,
    run_out,
    staged,
    fold,
):
    slabs = potential.shape[0]
    groups = run_out.shape[1]
    inverse = level_in[1]
    level = (level_in[0] - fold_row(mode_energy, fold.at[0])) * inverse
    damping = fold_row(broadening, fold.at[1]) * inverse
    for part in range(2):
        contact_out[part] = fold_row(self_left.at[0, part : part + 1], fold.at[2 + part]) * inverse
        contact_out[2 + part] = (
            fold_row(self_right.at[0, part : part + 1], fold.at[4 + part]) * inverse
        )
    onsite_out[slabs] = damping
    onsite_out[slabs + 1] = inverse
    width = profile.shape[2]
    depth = math.gcd(width, 256)
    block = math.gcd(groups, 2) * LANES
    totals = [None] * (groups * LANES // block)
    for start in range(0, width, depth):
        points = slice(start, start + depth)
        for place, total in enumerate(totals):
            rows = profile[0, place * block : (place + 1) * block, points]
            if place % 2:
                term = contract(rows, potential[:, points])
            else:
                term = contract(potential[:, points], rows)
            totals[place] = term if total is None else total + term
    for place, total in enumerate(totals):
        result = total.T if place % 2 else total
        for column in range(0, block, LANES):
            group = (place * block + column) // LANES
            staged[group * slabs : (group + 1) * slabs, :] = result[:, column : column + LANES]
    runs = []
    length = math.gcd(slabs, 4)
    for start in range(0, slabs, length):
        run = None
        for slab in range(start, start + length):
            real = level - staged[pl.ds(slab, groups, stride=slabs), :] * inverse
            onsite_out[slab] = real
            onsite = (real, damping)
            if run is None:
                alone = invert(onsite)
                run = (alone, alone, times(alone, alone))
            else:
                run = extend(run, onsite)
        runs.append(run)
    while len(runs) > 1:
        paired = [join(runs[k], runs[k + 1]) for k in range(0, len(runs) - 1, 2)]
        runs = paired + runs[2 * len(paired) :]
    for place, part in enumerate(part for pair in runs[0] for part in pair):
        run_out[place] = part


def multiply(half, profile, term, valleys, blocks, valley_shifts, block_shift):
    piece = term.shape[2]
    owner_block = lax.rem(lax.axis_index("blk") + block_shift, blocks)
    for place, shift in enumerate(valley_shifts):
        owner_valley = lax.rem(lax.axis_index("valley") + shift, valleys)
        start = pl.multiple_of((owner_valley * blocks + owner_block) * piece, piece)
        term[place] = jnp.dot(
            half[...], profile[0, :, pl.ds(start, piece)], preferred_element_type=jnp.float32
        )


def charge_kernel(
    reach,
    plan,
    occupation,
    onsite_in,
    outer_in,
    inner_run,
    sent_in,
    profile,
    charge,
    half,
    *rest,
):
    terms, staged = rest[:-1], rest[-1]
    slabs = charge.shape[1]
    groups = onsite_in.shape[1]
    outer = (outer_in[0], outer_in[1])
    inner = carry(
        tuple((inner_run[2 * k], inner_run[2 * k + 1]) for k in range(3)), (sent_in[0], sent_in[1])
    )
    is_upper = (lax.axis_index("slab") & reach) > 0
    left = pick(is_upper, inner, outer)
    right = pick(is_upper, outer, inner)
    damping = onsite_in[slabs]
    weight = (occupation[0] / math.pi) * onsite_in[slabs + 1]
    lefts, rights = [left], [right]
    for slab in range(slabs - 1):
        lefts.append(invert(minus((onsite_in[slab], damping), lefts[-1])))
        rights.append(invert(minus((onsite_in[slabs - 1 - slab], damping), rights[-1])))
    for slab in range(slabs):
        below = minus((onsite_in[slab], damping), plus(lefts[slab], rights[slabs - 1 - slab]))
        staged[pl.ds(slab, groups, stride=slabs), :] = (
            weight * below[1] / (below[0] * below[0] + below[1] * below[1])
        )
    for group in range(groups):
        columns = slice(group * LANES, (group + 1) * LANES)
        rows = staged[group * slabs : (group + 1) * slabs, :]
        charge[0, :, columns] = rows
        half[:, columns] = rows.astype(jnp.bfloat16)
    for term, block_shift in zip(terms, range(1, plan[1]), strict=True):
        multiply(half, profile, term, *plan, block_shift)


def term_kernel(plan, block_shifts, half, profile, *rest):
    for term, block_shift in zip(rest[-len(block_shifts) :], block_shifts, strict=True):
        multiply(half, profile, term, *plan, block_shift)


def store_kernel(plan, half, profile, charge, after, term, charge_hbm, leaving):
    copy = pltpu.make_async_copy(charge, charge_hbm, leaving)
    copy.start()
    multiply(half, profile, term, *plan, 0)
    copy.wait()


def alone_like(run):
    zero = jnp.zeros_like(run[0])
    return ((zero, zero), (zero, zero), (zero + 1.0, zero))


def widen(reach, group, other, before=None, after=None):
    is_second = (lax.axis_index("slab") & reach) > 0
    group, other = unpack(group), unpack(other)
    nothing = alone_like(group[0])
    if before is None:
        before, after = pick(is_second, other, nothing), pick(is_second, nothing, other)
    else:
        before, after = unpack(before), unpack(after)
        before, after = (
            pick(is_second, join(other, before), before),
            pick(is_second, after, join(after, other)),
        )
    group = join(pick(is_second, other, group), pick(is_second, group, other))
    return pack(group), pack(before), pack(after)


def close(reach, contact, group, before=None, after=None):
    is_upper = (lax.axis_index("slab") & reach) > 0
    group = unpack(group)
    nothing = alone_like(group[0])
    before = nothing if before is None else unpack(before)
    after = nothing if after is None else unpack(after)
    left_end, right_end = unpack(contact)
    end = pick(is_upper, right_end, left_end)
    sent = carry(pick(is_upper, flip(group), group), end)
    outer = carry(pick(is_upper, flip(after), before), end)
    inner_run = pick(is_upper, before, flip(after))
    return pack((sent,)), pack((outer,)), pack(inner_run)


def settle(reach, contact, *runs):
    return close(2 * reach, contact, *widen(reach, *runs))


def on_vmem(function, *arrays):
    def kernel(*refs):
        results = function(*(ref[...] for ref in refs[: len(arrays)]))
        for ref, result in zip(refs[len(arrays) :], results, strict=True):
            ref[...] = result

    shapes = jax.eval_shape(function, *arrays)
    vmem = pl.BlockSpec(memory_space=pltpu.VMEM)
    return pl.pallas_call(
        kernel,
        out_shape=shapes,
        in_specs=[vmem] * len(arrays),
        out_specs=jax.tree.map(lambda shape: vmem, shapes),
        compiler_params=pltpu.CompilerParams(vmem_limit_bytes=SMALL_LIMIT),
    )(*arrays)


def body(
    potential,
    mode_density,
    energy,
    hopping,
    mode_energy,
    broadening,
    self_left,
    self_right,
    occupation,
):
    slabs, width = potential.shape
    modes = mode_density.shape[1]
    groups = modes // LANES
    smem = pl.BlockSpec(memory_space=pltpu.SMEM)
    vmem = pl.BlockSpec(memory_space=pltpu.VMEM)
    anywhere = pl.BlockSpec(memory_space=pl.ANY)
    f32 = jnp.float32
    level = pl.pallas_call(
        scalar_kernel,
        out_shape=jax.ShapeDtypeStruct((2, groups, LANES), f32),
        in_specs=[smem, smem],
        out_specs=vmem,
        compiler_params=pltpu.CompilerParams(vmem_limit_bytes=SMALL_LIMIT),
        cost_estimate=pl.CostEstimate(
            flops=600 * width * modes, bytes_accessed=8, transcendentals=0
        ),
    )(energy, hopping)
    onsite, contact, run = pl.pallas_call(
        project_kernel,
        out_shape=(
            jax.ShapeDtypeStruct((slabs + 2, groups, LANES), f32),
            jax.ShapeDtypeStruct((4, groups, LANES), f32),
            jax.ShapeDtypeStruct((6, groups, LANES), f32),
        ),
        in_specs=[vmem] * 7,
        out_specs=(vmem, vmem, vmem),
        scratch_shapes=[
            pltpu.VMEM((groups * slabs, LANES), f32),
            pltpu.VMEM((6, groups, LANES), f32),
        ],
        compiler_params=pltpu.CompilerParams(vmem_limit_bytes=VMEM_LIMIT),
        cost_estimate=pl.CostEstimate(
            flops=2 * slabs * width * modes, bytes_accessed=2 * width * modes, transcendentals=0
        ),
    )(level, potential, mode_energy, broadening, self_left, self_right, mode_density)

    count = lax.axis_size("slab")
    around = ()
    group = run
    reach = 1
    while 2 * reach < count:
        other = lax.ppermute(group, "slab", [(k, k ^ reach) for k in range(count)])
        if 4 * reach < count:
            group, *around = on_vmem(functools.partial(widen, reach), group, other, *around)
        else:
            sent, outer, inner_run = on_vmem(
                functools.partial(settle, reach), contact, group, other, *around
            )
        reach *= 2
    if count <= 2:
        sent, outer, inner_run = on_vmem(functools.partial(close, reach), contact, group)
    if count > 1:
        sent = lax.ppermute(sent, "slab", [(k, k ^ reach) for k in range(count)])
    else:
        sent = contact[2:]

    valleys, blocks = lax.axis_size("valley"), lax.axis_size("blk")
    piece = width // (valleys * blocks)
    away_plan = (valleys, blocks, tuple(range(1, valleys)))
    home_plan = (valleys, blocks, (0,))

    def term_shapes(plan, count):
        return [jax.ShapeDtypeStruct((len(plan[2]), slabs, piece), f32)] * count

    def cost(plan, count, scale=1):
        columns = len(plan[2]) * count * piece // scale
        return pl.CostEstimate(
            flops=2 * slabs * columns * modes, bytes_accessed=2 * columns * modes, transcendentals=0
        )

    def swap(terms):
        return [
            lax.ppermute(term, "blk", [(k, (k + shift) % blocks) for k in range(blocks)])
            for shift, term in enumerate(terms, 1)
        ]

    first_plan = away_plan if valleys > 1 else home_plan
    charge, half, *others = pl.pallas_call(
        functools.partial(charge_kernel, reach, first_plan),
        out_shape=[
            jax.ShapeDtypeStruct((1, slabs, modes), f32),
            jax.ShapeDtypeStruct((slabs, modes), jnp.bfloat16),
        ]
        + term_shapes(first_plan, blocks - 1),
        in_specs=[smem] + [vmem] * 5,
        out_specs=[vmem] * (blocks + 1),
        scratch_shapes=[pltpu.VMEM((groups * slabs, LANES), f32)],
        compiler_params=pltpu.CompilerParams(vmem_limit_bytes=VMEM_LIMIT),
        cost_estimate=cost(first_plan, blocks - 1),
    )(occupation, onsite, outer, inner_run, sent, mode_density)

    def terms_of(plan, block_shifts, *after):
        return pl.pallas_call(
            functools.partial(term_kernel, plan, block_shifts),
            out_shape=term_shapes(plan, len(block_shifts)),
            in_specs=[vmem] * 2 + [anywhere] * len(after),
            out_specs=[vmem] * len(block_shifts),
            compiler_params=pltpu.CompilerParams(vmem_limit_bytes=VMEM_LIMIT),
            cost_estimate=cost(plan, len(block_shifts), 512),
        )(half, mode_density, *after)

    def send(terms, block_shift):
        received = []
        for shift in range(1, valleys):
            pairs = [
                (v * blocks + b, (v + shift) % valleys * blocks + (b + block_shift) % blocks)
                for v in range(valleys)
                for b in range(blocks)
            ]
            received.append(lax.ppermute(terms[shift - 1], ("valley", "blk"), pairs))
        return received

    arrived = []
    after = half
    if valleys > 1:
        straight = terms_of(away_plan, (0,))[0]
        arrived += send(straight, 0)
        for block_shift, term in enumerate(others, 1):
            arrived += send(term, block_shift)
        after = straight
        others = terms_of(home_plan, range(1, blocks), after) if blocks > 1 else []
    others = swap(others)
    term, charge = pl.pallas_call(
        functools.partial(store_kernel, home_plan),
        out_shape=term_shapes(home_plan, 1) + [jax.ShapeDtypeStruct(charge.shape, f32)],
        in_specs=[vmem] * 3 + [anywhere],
        out_specs=[vmem, anywhere],
        scratch_shapes=[pltpu.SemaphoreType.DMA],
        compiler_params=pltpu.CompilerParams(vmem_limit_bytes=VMEM_LIMIT),
        cost_estimate=cost(home_plan, 1, 512),
    )(half, mode_density, charge, after)
    density = term[0]
    for part in others:
        density = density + part[0]
    for part in arrived:
        density = density + part
    return charge, density


def solution(mesh):
    placed = (
        P("slab", None),
        P(("parts", "valley"), "blk", None),
        P(("parts", "valley")),
        P(("parts", "valley")),
        P(("parts", "valley"), "blk"),
        P(("parts", "valley"), "blk"),
        P(("parts", "valley"), None, "blk"),
        P(("parts", "valley"), None, "blk"),
        P(("parts", "valley")),
    )
    return jax.shard_map(
        body,
        mesh=mesh,
        in_specs=placed,
        out_specs=(P(("parts", "valley"), "slab", "blk"), P(("parts", "slab"), ("valley", "blk"))),
        check_vma=False,
    )
```

```python
import functools
import math

import jax
import jax.numpy as jnp
from jax import lax
from jax.experimental import pallas as pl
from jax.experimental.pallas import tpu as pltpu
from jax.sharding import PartitionSpec as P

LANES = 128
VMEM_LIMIT = 24 * 1024 * 1024
SMALL_LIMIT = 8 * 1024 * 1024


def times(first, second):
    return (
        first[0] * second[0] - first[1] * second[1],
        first[0] * second[1] + first[1] * second[0],
    )


def plus(first, second):
    return first[0] + second[0], first[1] + second[1]


def minus(first, second):
    return first[0] - second[0], first[1] - second[1]


def invert(value):
    scale = 1.0 / (value[0] * value[0] + value[1] * value[1])
    return value[0] * scale, -(value[1] * scale)


def one_minus(value):
    return 1.0 - value[0], -value[1]


def extend(run, slab):
    low, high, through = run
    grown = invert(minus(slab, high))
    return (
        plus(low, times(through, grown)),
        grown,
        times(through, times(grown, grown)),
    )


def join(first, second):
    low1, high1, through1 = first
    low2, high2, through2 = second
    bridge = invert(one_minus(times(high1, low2)))
    return (
        plus(low1, times(times(through1, low2), bridge)),
        plus(high2, times(times(through2, high1), bridge)),
        times(times(through1, through2), times(bridge, bridge)),
    )


def flip(run):
    return run[1], run[0], run[2]


def carry(run, value):
    low, high, through = run
    return plus(high, times(times(through, value), invert(one_minus(times(low, value)))))


def pick(flag, chosen, otherwise):
    return jax.tree.map(lambda a, b: jnp.where(flag, a, b), chosen, otherwise)


def pack(run):
    return jnp.stack([part for pair in run for part in pair])


def unpack(stack):
    return tuple((stack[2 * k], stack[2 * k + 1]) for k in range(stack.shape[0] // 2))


def fold_row(row, fold):
    for group in range(fold.shape[0]):
        fold[group : group + 1, :] = row[:, group * LANES : (group + 1) * LANES]
    return fold[...]


def contract(first, second):
    return lax.dot_general(
        first, second, (((1,), (1,)), ((), ())), preferred_element_type=jnp.float32
    )


def scalar_kernel(energy, hopping, level_out):
    level_out[0] = jnp.full(level_out.shape[1:], energy[0], jnp.float32)
    level_out[1] = 1.0 / jnp.full(level_out.shape[1:], hopping[0], jnp.float32)


def project_kernel(
    level_in,
    potential,
    mode_energy,
    broadening,
    self_left,
    self_right,
    profile,
    onsite_out,
    contact_out,
    run_out,
    staged,
    fold,
):
    slabs = potential.shape[0]
    groups = run_out.shape[1]
    inverse = level_in[1]
    level = (level_in[0] - fold_row(mode_energy, fold.at[0])) * inverse
    damping = fold_row(broadening, fold.at[1]) * inverse
    for part in range(2):
        contact_out[part] = fold_row(self_left.at[0, part : part + 1], fold.at[2 + part]) * inverse
        contact_out[2 + part] = (
            fold_row(self_right.at[0, part : part + 1], fold.at[4 + part]) * inverse
        )
    onsite_out[slabs] = damping
    onsite_out[slabs + 1] = inverse
    width = profile.shape[2]
    depth = math.gcd(width, 256)
    block = math.gcd(groups, 2) * LANES
    totals = [None] * (groups * LANES // block)
    for start in range(0, width, depth):
        points = slice(start, start + depth)
        for place, total in enumerate(totals):
            rows = profile[0, place * block : (place + 1) * block, points]
            if place % 2:
                term = contract(rows, potential[:, points])
            else:
                term = contract(potential[:, points], rows)
            totals[place] = term if total is None else total + term
    for place, total in enumerate(totals):
        result = total.T if place % 2 else total
        for column in range(0, block, LANES):
            group = (place * block + column) // LANES
            staged[group * slabs : (group + 1) * slabs, :] = result[:, column : column + LANES]
    runs = []
    length = math.gcd(slabs, 4)
    for start in range(0, slabs, length):
        run = None
        for slab in range(start, start + length):
            real = level - staged[pl.ds(slab, groups, stride=slabs), :] * inverse
            onsite_out[slab] = real
            onsite = (real, damping)
            if run is None:
                alone = invert(onsite)
                run = (alone, alone, times(alone, alone))
            else:
                run = extend(run, onsite)
        runs.append(run)
    while len(runs) > 1:
        paired = [join(runs[k], runs[k + 1]) for k in range(0, len(runs) - 1, 2)]
        runs = paired + runs[2 * len(paired) :]
    for place, part in enumerate(part for pair in runs[0] for part in pair):
        run_out[place] = part


def multiply(half, profile, term, valleys, blocks, valley_shifts, block_shift):
    piece = term.shape[2]
    owner_block = lax.rem(lax.axis_index("blk") + block_shift, blocks)
    for place, shift in enumerate(valley_shifts):
        owner_valley = lax.rem(lax.axis_index("valley") + shift, valleys)
        start = pl.multiple_of((owner_valley * blocks + owner_block) * piece, piece)
        term[place] = jnp.dot(
            half[...], profile[0, :, pl.ds(start, piece)], preferred_element_type=jnp.float32
        )


def charge_kernel(
    reach,
    plan,
    block_shifts,
    occupation,
    onsite_in,
    outer_in,
    inner_run,
    sent_in,
    profile,
    charge,
    half,
    *rest,
):
    terms, staged = rest[:-1], rest[-1]
    slabs = charge.shape[1]
    groups = onsite_in.shape[1]
    outer = (outer_in[0], outer_in[1])
    inner = carry(
        tuple((inner_run[2 * k], inner_run[2 * k + 1]) for k in range(3)), (sent_in[0], sent_in[1])
    )
    is_upper = (lax.axis_index("slab") & reach) > 0
    left = pick(is_upper, inner, outer)
    right = pick(is_upper, outer, inner)
    damping = onsite_in[slabs]
    weight = (occupation[0] / math.pi) * onsite_in[slabs + 1]
    lefts, rights = [left], [right]
    for slab in range(slabs - 1):
        lefts.append(invert(minus((onsite_in[slab], damping), lefts[-1])))
        rights.append(invert(minus((onsite_in[slabs - 1 - slab], damping), rights[-1])))
    for slab in range(slabs):
        below = minus((onsite_in[slab], damping), plus(lefts[slab], rights[slabs - 1 - slab]))
        staged[pl.ds(slab, groups, stride=slabs), :] = (
            weight * below[1] / (below[0] * below[0] + below[1] * below[1])
        )
    for group in range(groups):
        columns = slice(group * LANES, (group + 1) * LANES)
        rows = staged[group * slabs : (group + 1) * slabs, :]
        charge[0, :, columns] = rows
        half[:, columns] = rows.astype(jnp.bfloat16)
    for term, block_shift in zip(terms, block_shifts, strict=True):
        multiply(half, profile, term, *plan, block_shift)


def term_kernel(plan, block_shifts, half, profile, *rest):
    for term, block_shift in zip(rest[-len(block_shifts) :], block_shifts, strict=True):
        multiply(half, profile, term, *plan, block_shift)


def store_kernel(plan, half, profile, charge, after, term, charge_hbm, leaving):
    copy = pltpu.make_async_copy(charge, charge_hbm, leaving)
    copy.start()
    multiply(half, profile, term, *plan, 0)
    copy.wait()


def alone_like(run):
    zero = jnp.zeros_like(run[0])
    return ((zero, zero), (zero, zero), (zero + 1.0, zero))


def widen(reach, group, other, before=None, after=None):
    is_second = (lax.axis_index("slab") & reach) > 0
    group, other = unpack(group), unpack(other)
    nothing = alone_like(group[0])
    if before is None:
        before, after = pick(is_second, other, nothing), pick(is_second, nothing, other)
    else:
        before, after = unpack(before), unpack(after)
        before, after = (
            pick(is_second, join(other, before), before),
            pick(is_second, after, join(after, other)),
        )
    group = join(pick(is_second, other, group), pick(is_second, group, other))
    return pack(group), pack(before), pack(after)


def close(reach, contact, group, before=None, after=None):
    is_upper = (lax.axis_index("slab") & reach) > 0
    group = unpack(group)
    nothing = alone_like(group[0])
    before = nothing if before is None else unpack(before)
    after = nothing if after is None else unpack(after)
    left_end, right_end = unpack(contact)
    end = pick(is_upper, right_end, left_end)
    sent = carry(pick(is_upper, flip(group), group), end)
    outer = carry(pick(is_upper, flip(after), before), end)
    inner_run = pick(is_upper, before, flip(after))
    return pack((sent,)), pack((outer,)), pack(inner_run)


def settle(reach, contact, *runs):
    return close(2 * reach, contact, *widen(reach, *runs))


def on_vmem(function, *arrays):
    def kernel(*refs):
        results = function(*(ref[...] for ref in refs[: len(arrays)]))
        for ref, result in zip(refs[len(arrays) :], results, strict=True):
            ref[...] = result

    shapes = jax.eval_shape(function, *arrays)
    vmem = pl.BlockSpec(memory_space=pltpu.VMEM)
    return pl.pallas_call(
        kernel,
        out_shape=shapes,
        in_specs=[vmem] * len(arrays),
        out_specs=jax.tree.map(lambda shape: vmem, shapes),
        compiler_params=pltpu.CompilerParams(vmem_limit_bytes=SMALL_LIMIT),
    )(*arrays)


def body(
    potential,
    mode_density,
    energy,
    hopping,
    mode_energy,
    broadening,
    self_left,
    self_right,
    occupation,
):
    slabs, width = potential.shape
    modes = mode_density.shape[1]
    groups = modes // LANES
    smem = pl.BlockSpec(memory_space=pltpu.SMEM)
    vmem = pl.BlockSpec(memory_space=pltpu.VMEM)
    anywhere = pl.BlockSpec(memory_space=pl.ANY)
    f32 = jnp.float32
    level = pl.pallas_call(
        scalar_kernel,
        out_shape=jax.ShapeDtypeStruct((2, groups, LANES), f32),
        in_specs=[smem, smem],
        out_specs=vmem,
        compiler_params=pltpu.CompilerParams(vmem_limit_bytes=SMALL_LIMIT),
        cost_estimate=pl.CostEstimate(
            flops=600 * width * modes, bytes_accessed=8, transcendentals=0
        ),
    )(energy, hopping)
    onsite, contact, run = pl.pallas_call(
        project_kernel,
        out_shape=(
            jax.ShapeDtypeStruct((slabs + 2, groups, LANES), f32),
            jax.ShapeDtypeStruct((4, groups, LANES), f32),
            jax.ShapeDtypeStruct((6, groups, LANES), f32),
        ),
        in_specs=[vmem] * 7,
        out_specs=(vmem, vmem, vmem),
        scratch_shapes=[
            pltpu.VMEM((groups * slabs, LANES), f32),
            pltpu.VMEM((6, groups, LANES), f32),
        ],
        compiler_params=pltpu.CompilerParams(vmem_limit_bytes=VMEM_LIMIT),
        cost_estimate=pl.CostEstimate(
            flops=2 * slabs * width * modes, bytes_accessed=2 * width * modes, transcendentals=0
        ),
    )(level, potential, mode_energy, broadening, self_left, self_right, mode_density)

    count = lax.axis_size("slab")
    around = ()
    group = run
    reach = 1
    while 2 * reach < count:
        other = lax.ppermute(group, "slab", [(k, k ^ reach) for k in range(count)])
        if 4 * reach < count:
            group, *around = on_vmem(functools.partial(widen, reach), group, other, *around)
        else:
            sent, outer, inner_run = on_vmem(
                functools.partial(settle, reach), contact, group, other, *around
            )
        reach *= 2
    if count <= 2:
        sent, outer, inner_run = on_vmem(functools.partial(close, reach), contact, group)
    if count > 1:
        sent = lax.ppermute(sent, "slab", [(k, k ^ reach) for k in range(count)])
    else:
        sent = contact[2:]

    valleys, blocks = lax.axis_size("valley"), lax.axis_size("blk")
    piece = width // (valleys * blocks)
    away_plan = (valleys, blocks, tuple(range(1, valleys)))
    home_plan = (valleys, blocks, (0,))

    def term_shapes(plan, count):
        return [jax.ShapeDtypeStruct((len(plan[2]), slabs, piece), f32)] * count

    def cost(plan, count, scale=1):
        columns = len(plan[2]) * count * piece // scale
        return pl.CostEstimate(
            flops=2 * slabs * columns * modes, bytes_accessed=2 * columns * modes, transcendentals=0
        )

    def swap(terms):
        return [
            lax.ppermute(term, "blk", [(k, (k + shift) % blocks) for k in range(blocks)])
            for shift, term in enumerate(terms, 1)
        ]

    first_plan = away_plan if valleys > 1 else home_plan
    first_shifts = [*range(1, blocks)] + [0] * (valleys > 1)
    charge, half, *others = pl.pallas_call(
        functools.partial(charge_kernel, reach, first_plan, first_shifts),
        out_shape=[
            jax.ShapeDtypeStruct((1, slabs, modes), f32),
            jax.ShapeDtypeStruct((slabs, modes), jnp.bfloat16),
        ]
        + term_shapes(first_plan, len(first_shifts)),
        in_specs=[smem] + [vmem] * 5,
        out_specs=[vmem] * (2 + len(first_shifts)),
        scratch_shapes=[pltpu.VMEM((groups * slabs, LANES), f32)],
        compiler_params=pltpu.CompilerParams(vmem_limit_bytes=VMEM_LIMIT),
        cost_estimate=cost(first_plan, len(first_shifts)),
    )(occupation, onsite, outer, inner_run, sent, mode_density)

    def terms_of(plan, block_shifts, *after):
        return pl.pallas_call(
            functools.partial(term_kernel, plan, block_shifts),
            out_shape=term_shapes(plan, len(block_shifts)),
            in_specs=[vmem] * 2 + [anywhere] * len(after),
            out_specs=[vmem] * len(block_shifts),
            compiler_params=pltpu.CompilerParams(vmem_limit_bytes=VMEM_LIMIT),
            cost_estimate=cost(plan, len(block_shifts), 512),
        )(half, mode_density, *after)

    def send(terms, block_shift):
        received = []
        for shift in range(1, valleys):
            pairs = [
                (v * blocks + b, (v + shift) % valleys * blocks + (b + block_shift) % blocks)
                for v in range(valleys)
                for b in range(blocks)
            ]
            received.append(lax.ppermute(terms[shift - 1], ("valley", "blk"), pairs))
        return received

    arrived = []
    after = half
    if valleys > 1:
        for block_shift, term in reversed([*zip(first_shifts, others, strict=True)]):
            arrived += send(term, block_shift)
        after = others[-1]
        others = terms_of(home_plan, range(1, blocks), after) if blocks > 1 else []
    others = swap(others)
    term, charge = pl.pallas_call(
        functools.partial(store_kernel, home_plan),
        out_shape=term_shapes(home_plan, 1) + [jax.ShapeDtypeStruct(charge.shape, f32)],
        in_specs=[vmem] * 3 + [anywhere],
        out_specs=[vmem, anywhere],
        scratch_shapes=[pltpu.SemaphoreType.DMA],
        compiler_params=pltpu.CompilerParams(vmem_limit_bytes=VMEM_LIMIT),
        cost_estimate=cost(home_plan, 1, 512),
    )(half, mode_density, charge, after)
    density = term[0]
    for part in others:
        density = density + part[0]
    for part in arrived:
        density = density + part
    return charge, density


def solution(mesh):
    placed = (
        P("slab", None),
        P(("parts", "valley"), "blk", None),
        P(("parts", "valley")),
        P(("parts", "valley")),
        P(("parts", "valley"), "blk"),
        P(("parts", "valley"), "blk"),
        P(("parts", "valley"), None, "blk"),
        P(("parts", "valley"), None, "blk"),
        P(("parts", "valley")),
    )
    return jax.shard_map(
        body,
        mesh=mesh,
        in_specs=placed,
        out_specs=(P(("parts", "valley"), "slab", "blk"), P(("parts", "slab"), ("valley", "blk"))),
        check_vma=False,
    )
```
